32 devices in a mesh: dp: 4 (over z), expert: 8 (over y, x, core).
Axes of the slice: x: 2, y: 2, z: 4, core: 2. Of those that a mesh axis runs over, the one named last changes fastest.
Arguments:
- grad_out: bfloat16 [4096, 2880], P(('dp', 'expert')), may hold values from -96 to 96
- hidden_act: bfloat16 [4096, 4, 360], P(('dp', 'expert')), may hold values from -6 to 6
- gate_weights: bfloat16 [4096, 4], P(('dp', 'expert')), may hold values from 0.099609375 to 0.69921875
- routing: int32 [4096, 4], P(('dp', 'expert')), may hold values from 0 to 7, all different within a row; in each aligned block of 128 rows (0 to 127, 128 to 255, ...) at most 80 rows name the same one
- resp_lengths: int32 [32, 4], P(('dp', 'expert')), may hold values from 1 to 64, 128 in all within a row
- advantage: float32 [32, 4], P(('dp', 'expert')), may hold values from -4 to 4
- w_down: bfloat16 [8, 360, 2880], P('expert', None, 'dp'), may hold values from -0.3125 to 0.3125
Outputs:
- grad_down: float32 [8, 360, 2880], P('expert', None, 'dp')
- grad_hidden: float32 [4096, 4, 360], P(('dp', 'expert'))
- grad_gates: float32 [4096, 4], P(('dp', 'expert'))
The draws below stay inside these ranges and needn't reach their ends.
Inputs may be any that keep to these rules, and one draw needn't show every extreme that they name: `routing`: each token names 4 different experts; within the 128 tokens of one device no expert is named more than 80 times, a bound that some block reaches. `resp_lengths`: the 4 lengths of one device add up to 128; the largest is 64.
All inputs are finite; a program needn't handle non-finite values.
Results may differ from the reference program's by a relative error of at most 0.0041.
Values may be sent and summed in bfloat16 or wider, within the bound.
A program may use at most 64 MiB of HBM per device.

```python
import math
import jax
import jax.numpy as jnp
import numpy as np
from jax import lax

D = 2880
TOPK = 4
FFW = 360
ROWS = 128
SEQ_DEV = 4
EXPERTS = 8
CAP = 80
LMAX = 64
TOKENS = 4096
N_DP = 4
N_EXPERT = 8


def spiked(entries, own_key, source, target, shards_of, factor):
    owner, partner = [(jnp.arange(entries.shape[dim]) // (entries.shape[dim] // shards_of)).reshape([-1 if axis == dim else 1 for axis in range(entries.ndim)]) for dim in (source, target)]
    chosen = jax.random.permutation(own_key, shards_of)[partner]
    strong = (owner == chosen) | (owner == (partner + shards_of // 2) % shards_of)
    return jnp.where(strong, factor * entries, entries)


def level_of(rng, dims, shards, least, top_value):
    def one(dim, shards_of):
        draws = jax.random.uniform(jax.random.fold_in(jax.random.fold_in(rng, 6), dim), (shards_of,), jnp.float32, least / len(shards), top_value / len(shards))
        return jnp.repeat(jnp.exp(draws), dims[dim] // shards_of).reshape((-1,) + (1,) * (len(dims) - dim - 1))

    level = one(*shards[0])
    for cut in shards[1:]:
        level = level * one(*cut)
    return level


def profile(count, total, most, slope):
    loads = [(1 << 20) // math.isqrt(grade ** slope) + 1 for grade in range(2, count + 1)]
    spare, given = total - most - (count - 1), [1] * (count - 1)
    while spare > 0:
        candidates = [i for i in range(count - 1) if given[i] < most]
        pool, left = sum([loads[i] for i in candidates]), spare
        for i in candidates:
            more = min(most - given[i], max(1, left * loads[i] // pool), spare)
            given[i] = given[i] + more
            spare = spare - more
    return np.array([most] + given)


def ragged(stream_key, amount, total, bound, slope):
    if amount == 2:
        one = jax.random.randint(stream_key, (), max(1, total - bound), min(bound, total - 1) + 1)
        return jnp.stack([one, total - one])
    lengths = jnp.asarray(profile(amount, total, bound, slope), jnp.int32)
    pairs = (amount - 1) // 2
    giver, taker = lengths[1:1 + 2 * pairs:2], lengths[2:2 + 2 * pairs:2]
    margin = jnp.minimum(giver - 1, bound - taker)
    shifted = jax.random.randint(jax.random.fold_in(stream_key, 1), (pairs,), 0, 1 << 20) % (margin + 1)
    lengths = lengths.at[1:1 + 2 * pairs:2].set(giver - shifted).at[2:2 + 2 * pairs:2].set(taker + shifted)
    return lengths[jax.random.permutation(jax.random.fold_in(stream_key, 2), amount)]


def shared_out(rng, own, number, rows, amount, top, reach, skew):
    ranking = jax.random.permutation(rng, amount)
    packed, common = shares(amount, rows * top, reach, skew, True), shares(amount, rows * top, reach, skew, False)
    places = jnp.arange(amount)

    def named(sizes, turn):
        used = int((sizes > 0).sum())
        fixed = max(1, used // 4)
        shifted = fixed + (places - fixed + turn * (used - fixed)) % max(1, amount - fixed)
        return jnp.zeros((amount,), jnp.int32).at[ranking[jnp.where(places < fixed, places, shifted)]].set(jnp.asarray(sizes, jnp.int32))

    sizes = jnp.where(number % 4 == 0, named(packed, number // 4), named(common, number - number // 4 - 1))
    mixed = jax.random.permutation(jax.random.fold_in(own, 3), amount)
    source_of, receiver = mixed[0:amount // 2 * 2:2], mixed[1:amount // 2 * 2:2]
    room = jnp.minimum(sizes[source_of] - 1, reach - sizes[receiver]) // 2
    room = jnp.where((source_of == ranking[0]) | (receiver == ranking[0]) | (sizes[receiver] == 0), 0, jnp.maximum(room, 0))
    shifted = jax.random.randint(jax.random.fold_in(own, 4), (amount // 2,), 0, 1 << 20) % (room + 1)
    sizes = sizes.at[source_of].add(-shifted).at[receiver].add(shifted)
    labels = jnp.searchsorted(jnp.cumsum(sizes), jnp.arange(rows * top), side="right").astype(jnp.int32)
    grid = labels.reshape(top, rows).T
    grid = grid[jax.random.permutation(jax.random.fold_in(own, 1), rows)]
    turn = jax.random.randint(jax.random.fold_in(own, 2), (rows, 1), 0, top)
    return jnp.take_along_axis(grid, (jnp.arange(top)[None, :] + turn) % top, axis=1)


def shares(count, total, limit, slope, full):
    weights = [(1 << 20) // math.isqrt(rank ** slope) + 1 for rank in range(1, count + 1)]
    largest = limit if full else min(limit, max(-(-total // count), total * weights[0] // sum(weights)))
    least = 1 if total - largest >= count - 1 else 0
    given, spare = [largest] + [least] * (count - 1), total - largest - least * (count - 1)
    while spare > 0:
        free = [i for i in range(1, count) if given[i] < largest] or [i for i in range(1, count) if given[i] < limit]
        whole, budget = sum([weights[i] for i in free]), spare
        for i in free:
            more = min(limit - given[i], max(1, budget * weights[i] // whole), spare)
            given[i] = given[i] + more
            spare = spare - more
    return np.array(given)


def normal_values(rng, dims, spread, bound, cuts=(), held_as=jnp.bfloat16):
    level = level_of(rng, dims, cuts, -0.22, 0.18) if cuts else 1.0
    drawn = jax.random.normal(rng, dims, jnp.float32) * spread * level
    return jnp.minimum(jnp.maximum(drawn, -bound), bound).astype(held_as)


def heavy_noise(key, shape, deviation, limit, split, heavy, kind=jnp.bfloat16):
    values = deviation * jax.random.normal(key, shape, jnp.float32)
    if split:
        values = values * level_of(key, shape, split, -0.22, 0.18)
    return jnp.clip(spiked(values, jax.random.fold_in(key, 3), *heavy), -limit, limit).astype(kind)


def setup_inputs(seed: int = 0) -> dict:
    seeds = jax.random.split(jax.random.key(seed), 8)
    grad_out = heavy_noise(seeds[0], (TOKENS, D), 16.0, 96.0, ((0, 32),), (0, 1, 32, 2.75))
    hidden_act = normal_values(seeds[1], (TOKENS, TOPK, FFW), 1.0, 6.0, ((0, 32),))
    gate_weights = jnp.clip(0.099609375 + 0.5996094 * jax.random.uniform(seeds[2], (TOKENS, TOPK), jnp.float32) ** level_of(seeds[2], (TOKENS, TOPK), ((0, 32),), -0.2, 0.2), 0.099609375, 0.69921875).astype(jnp.bfloat16)
    routing_keys = jax.random.split(jax.random.fold_in(seeds[3], 1), TOKENS // ROWS)
    routing_turns = jax.random.permutation(jax.random.fold_in(seeds[3], 3), TOKENS // ROWS)
    routing = jax.vmap(lambda own, number: shared_out(jax.random.fold_in(seeds[3], 2), own, number, ROWS, EXPERTS, TOPK, CAP, 2))(routing_keys, routing_turns).reshape((TOKENS, TOPK))
    resp_lengths = jax.vmap(lambda own: ragged(own, SEQ_DEV, ROWS, LMAX, 2))(jax.random.split(seeds[4], (N_DP * N_EXPERT))).reshape((N_DP * N_EXPERT, SEQ_DEV)).astype(jnp.int32)
    advantage = normal_values(seeds[5], (N_DP * N_EXPERT, SEQ_DEV), 1.0, 4.0, ((0, 32),), jnp.float32)
    w_down = normal_values(seeds[6], (EXPERTS, FFW, D), FFW ** -0.5, 0.3125, ((0, 8), (2, 4)))
    return dict(grad_out=grad_out, hidden_act=hidden_act, gate_weights=gate_weights, routing=routing, resp_lengths=resp_lengths, advantage=advantage, w_down=w_down)


def token_scale(resp_lengths, advantage):
    ends = jnp.cumsum(resp_lengths, axis=1).astype(jnp.int32)
    starts = (ends - resp_lengths).astype(jnp.int32)
    position = jnp.arange(ROWS, dtype=jnp.int32)
    inside = (position[None, :, None] >= starts[:, None, :]) & (position[None, :, None] < ends[:, None, :])
    ratio = advantage / resp_lengths.astype(advantage.dtype)
    return jnp.sum(jnp.where(inside, ratio[:, None, :], jnp.zeros((), advantage.dtype)), axis=2).reshape(-1)


def reference(grad_out, hidden_act, gate_weights, routing, resp_lengths, advantage, w_down):
    ftype = advantage.dtype
    scale = token_scale(resp_lengths, advantage)
    cotan = (scale[:, None] * grad_out.astype(ftype)).astype(jnp.bfloat16)
    items = TOKENS * TOPK
    dest = routing.reshape(-1).astype(jnp.int32)
    order = jnp.argsort(dest, stable=True).astype(jnp.int32)
    counts = jnp.sum((dest[:, None] == jnp.arange(EXPERTS, dtype=jnp.int32)[None, :]).astype(jnp.int32), axis=0).astype(jnp.int32)
    firsts = (jnp.cumsum(counts) - counts).astype(jnp.int32)
    padded = min(items, N_DP * N_EXPERT * CAP)
    order_pad = jnp.concatenate([order, jnp.full((padded,), items, jnp.int32)])
    hidden = hidden_act.reshape(items, FFW)
    gates = gate_weights.reshape(items)

    def per_expert(expert_id):
        index = lax.dynamic_slice_in_dim(order_pad, firsts[expert_id], padded)
        valid = jnp.arange(padded, dtype=jnp.int32) < counts[expert_id]
        index = jnp.where(valid, index, items).astype(jnp.int32)
        safe = jnp.minimum(index, items - 1).astype(jnp.int32)
        cot_rows = jnp.where(valid[:, None], cotan[safe // TOPK].astype(ftype), jnp.zeros((), ftype))
        hid_rows = jnp.where(valid[:, None], hidden[safe].astype(ftype), jnp.zeros((), ftype))
        gate_rows = gates[safe].astype(ftype)
        gated = (gate_rows[:, None] * cot_rows).astype(jnp.bfloat16)
        gated = lax.optimization_barrier(gated).astype(ftype)
        weight = w_down[expert_id].astype(ftype)
        dweight = jnp.dot(hid_rows.T, gated)
        back = jnp.dot(cot_rows, weight.T)
        dhid = gate_rows[:, None] * back
        output = jnp.dot(hid_rows, weight)
        dgate = jnp.sum(cot_rows * output, axis=1)
        return dweight, dhid, dgate, index

    grad_down, dhid, dgate, index = lax.map(per_expert, jnp.arange(EXPERTS, dtype=jnp.int32))
    flat_index = index.reshape(-1)
    grad_hidden = jnp.zeros((items, FFW), ftype).at[flat_index].set(dhid.reshape(-1, FFW), mode="drop")
    grad_gates = jnp.zeros((items,), ftype).at[flat_index].set(dgate.reshape(-1), mode="drop")
    return grad_down, grad_hidden.reshape(TOKENS, TOPK, FFW), grad_gates.reshape(TOKENS, TOPK)
```

```python
import functools

import jax
import jax.numpy as jnp
from jax import lax
from jax.experimental import pallas as pl
from jax.experimental.pallas import tpu as pltpu
from jax.sharding import PartitionSpec as P


def weight_terms(hid_recv, gated):
    partial_term = lax.dot_general(
        hid_recv, gated, (((0,), (0,)), ((), ())), preferred_element_type=jnp.float32
    )
    return lax.psum_scatter(partial_term, "dp", scatter_dimension=1, tiled=True)[None]


def local(grad_out, hidden_act, gate_weights, routing, resp_lengths, advantage, w_down):
    rows = grad_out.shape[0]
    width = grad_out.shape[1]
    topk = routing.shape[1]
    ffw = hidden_act.shape[2]
    nexp = lax.axis_size("expert")
    cap = min(rows, 5 * rows * topk // (4 * nexp))
    items = rows * topk
    slots = nexp * cap
    ends = jnp.cumsum(resp_lengths[0])
    starts = ends - resp_lengths[0]
    position = jnp.arange(rows, dtype=jnp.int32)
    inside = (position[:, None] >= starts[None, :]) & (position[:, None] < ends[None, :])
    ratio = advantage[0] / resp_lengths[0].astype(jnp.float32)
    scale = jnp.sum(jnp.where(inside, ratio[None, :], 0.0), axis=1)
    cotan = (scale[:, None] * grad_out.astype(jnp.float32)).astype(jnp.bfloat16)
    dest = routing.reshape(-1)
    onehot = (dest[:, None] == jnp.arange(nexp, dtype=jnp.int32)[None, :]).astype(jnp.int32)
    rank = jnp.cumsum(onehot, axis=0) - onehot
    place = jnp.sum(rank * onehot, axis=1)
    flat = dest * cap + place
    slot_item = (
        jnp.full((slots,), items, jnp.int32).at[flat].set(jnp.arange(items, dtype=jnp.int32))
    )
    valid = slot_item < items
    safe = jnp.minimum(slot_item, items - 1)
    send_cot = jnp.where(valid[:, None], cotan[safe // topk], jnp.zeros((), jnp.bfloat16))
    send_hid = jnp.where(
        valid[:, None], hidden_act.reshape(items, ffw)[safe], jnp.zeros((), jnp.bfloat16)
    )
    send_gate = jnp.where(valid, gate_weights.reshape(items)[safe], jnp.zeros((), jnp.bfloat16))
    recv_cot, recv_hid, recv_gate = (
        lax.all_to_all(
            send_cot.reshape(nexp, cap, width), "expert", split_axis=0, concat_axis=0, tiled=True
        ),
        lax.all_to_all(
            send_hid.reshape(nexp, cap, ffw), "expert", split_axis=0, concat_axis=0, tiled=True
        ),
        lax.all_to_all(
            send_gate.reshape(nexp, cap), "expert", split_axis=0, concat_axis=0, tiled=True
        ),
    )
    recv_cot = recv_cot.reshape(slots, width)
    recv_hid = recv_hid.reshape(slots, ffw)
    recv_gate = recv_gate.reshape(slots).astype(jnp.float32)
    gated = (recv_gate[:, None] * recv_cot.astype(jnp.float32)).astype(jnp.bfloat16)
    local_weight = w_down[0]
    piece = lax.all_gather(local_weight, "dp", axis=1, tiled=True)
    back_sum = lax.dot_general(
        recv_cot, piece, (((1,), (1,)), ((), ())), preferred_element_type=jnp.float32
    )
    output = jnp.dot(recv_hid, piece, preferred_element_type=jnp.float32)
    gate_sum = jnp.sum(recv_cot.astype(jnp.float32) * output, axis=1)
    dhid = recv_gate[:, None] * back_sum
    result_hid, result_gate = (
        lax.all_to_all(
            dhid.reshape(nexp, cap, ffw), "expert", split_axis=0, concat_axis=0, tiled=True
        ),
        lax.all_to_all(
            gate_sum.reshape(nexp, cap), "expert", split_axis=0, concat_axis=0, tiled=True
        ),
    )
    grad_down = weight_terms(recv_hid, gated)
    grad_hidden = result_hid.reshape(slots, ffw)[flat].reshape(rows, topk, ffw)
    grad_gates = result_gate.reshape(slots)[flat].reshape(rows, topk)
    return (grad_down, grad_hidden, grad_gates)


MESH = pl.DeviceIdType.MESH
SIB, ALONG_X, ALONG_Y = 1, 2, 4


def round_up(size, unit):
    return -(-size // unit) * unit


def token_scale(resp_lengths, advantage, rows):
    ends = jnp.cumsum(resp_lengths[0])
    starts = ends - resp_lengths[0]
    position = jnp.arange(rows, dtype=jnp.int32)
    inside = (position[:, None] >= starts[None, :]) & (position[:, None] < ends[None, :])
    ratio = advantage[0] / resp_lengths[0].astype(jnp.float32)
    return jnp.sum(jnp.where(inside, ratio[None, :], 0.0), axis=1)


def exchange_kernel(
    parts, cot_ref, gh_ref, w_ref, gd_ref, backr_ref,
    cg, ghr, ght, wfull, part, sendbuf, from_left, from_right, backs,
    c_send, c_recv, g_send, g_recv, w_send, w_recv, r_send, r_recv, b_send, b_recv,
):
    z = lax.axis_index("dp")
    e = lax.axis_index("expert")
    core, xpos, ypos = e % 2, (e // 2) % 2, e // 4
    last = parts - 1
    rows = cot_ref.shape[1]
    half = rows // 2
    low = 2 * z < parts

    def peer(mask):
        c = 1 - core if mask & 1 else core
        x = 1 - xpos if mask & 2 else xpos
        y = 1 - ypos if mask & 4 else ypos
        return (y * 2 + x) * 2 + c

    barrier = pltpu.get_barrier_semaphore()
    for mask in range(1, 8):
        pl.semaphore_signal(barrier, inc=1, device_id=(z, peer(mask)), device_id_type=MESH)

    @pl.when(z > 0)
    def _():
        pl.semaphore_signal(barrier, inc=1, device_id=(z - 1, e), device_id_type=MESH)

    @pl.when(z < last)
    def _():
        pl.semaphore_signal(barrier, inc=1, device_id=(z + 1, e), device_id_type=MESH)

    pl.semaphore_wait(barrier, 7 + jnp.minimum(z, 1) + jnp.minimum(last - z, 1))

    def remote(src, dst, send, recv, device):
        return pltpu.make_async_remote_copy(
            src_ref=src, dst_ref=dst, send_sem=send, recv_sem=recv,
            device_id=device, device_id_type=MESH,
        )

    def w_copy(hop, rightward):
        origin = z - hop if rightward else z + hop
        side = 0 if rightward else 1
        src = w_ref if hop == 0 else wfull.at[origin]
        target = z + 1 if rightward else z - 1
        return remote(
            src, wfull.at[origin], w_send.at[side, hop], w_recv.at[side, hop], (target, e)
        )

    def w_recv_wait(hop, rightward):
        origin = z - 1 - hop if rightward else z + 1 + hop
        side = 0 if rightward else 1
        remote(
            w_ref, wfull.at[origin], w_send.at[side, hop], w_recv.at[side, hop], (z, peer(SIB))
        ).wait_recv()

    def w_step(hop):
        for rightward in (True, False):
            if hop > 0:
                come = z >= hop if rightward else z + hop <= last

                @pl.when(come)
                def _(rightward=rightward):
                    w_recv_wait(hop - 1, rightward)

            if hop < last:
                go = (z >= hop) & (z < last) if rightward else (z + hop <= last) & (z > 0)

                @pl.when(go)
                def _(rightward=rightward):
                    w_copy(hop, rightward).start()

    def g_copy(mask):
        p = peer(mask)
        return remote(gh_ref.at[p], ghr.at[e], g_send.at[mask], g_recv.at[mask], (z, p))

    def chunk_of(step):
        return jnp.where(low, (z + parts - 1 - step) % parts, (z + 1 + step) % parts)

    def c_own(step, kind, mask):
        c = chunk_of(step)
        return remote(
            cot_ref.at[c], cg.at[c, e], c_send.at[step, kind], c_recv.at[step, kind],
            (z, peer(mask)),
        )

    def c_pass(step, kind, source, mask, first=None):
        c = chunk_of(step)
        ref = cg.at[c, peer(source)]
        if first is not None:
            ref = cg.at[c, peer(source), pl.ds(first, half)]
        return remote(
            ref, ref, c_send.at[step, kind], c_recv.at[step, kind], (z, peer(mask))
        )

    def c_copies(step):
        return [
            c_own(step, 0, SIB), c_own(step, 1, ALONG_X), c_own(step, 2, ALONG_Y),
            c_pass(step, 3, ALONG_X, ALONG_Y, 0),
            c_pass(step, 4, ALONG_Y, ALONG_X, half),
            c_pass(step, 5, ALONG_X, SIB), c_pass(step, 6, ALONG_Y, SIB),
            c_pass(step, 7, ALONG_X | ALONG_Y, SIB),
        ]

    copies = [c_copies(step) for step in range(parts)]

    w_step(0)
    for mask in (6, 2, 4, 1, 3, 5, 7):
        g_copy(mask).start()
    for kind in (1, 2, 0):
        copies[0][kind].start()
    ghr[e] = gh_ref[e]
    wfull[z] = w_ref[...]
    for c in range(parts):
        cg[c, e] = cot_ref[c]

    def gather(step):
        for kind in (1, 2):
            copies[step][kind].wait_recv()
        for kind in (3, 4):
            copies[step][kind].start()
        if step + 1 < parts:
            for kind in (1, 2, 0):
                copies[step + 1][kind].start()
        for kind in (5, 6):
            copies[step][kind].start()
        for kind in (3, 4):
            copies[step][kind].wait_recv()
        copies[step][7].start()
        for kind in (0, 5, 6, 7):
            copies[step][kind].wait_recv()

    def r_copy(c, rightward):
        side = 0 if rightward else 1
        dst = from_left if rightward else from_right
        return remote(
            sendbuf.at[c], dst.at[c], r_send.at[side, c], r_recv.at[side, c],
            (z + 1 if rightward else z - 1, e),
        )

    def r_wait(c, rightward):
        side = 0 if rightward else 1
        dst = from_left if rightward else from_right
        remote(
            sendbuf.at[c], dst.at[c], r_send.at[side, c], r_recv.at[side, c], (z, peer(SIB))
        ).wait_recv()

    def r_pass(c, rightward):
        r_wait(c, rightward)
        came = (from_left if rightward else from_right)[c].astype(jnp.float32)
        sendbuf[c] = (part[c] + came).astype(sendbuf.dtype)
        r_copy(c, rightward).start()

    middle = (z > 0) & (z < last)

    for step in range(parts):
        gather(step)
        if step == 0:
            for mask in range(1, 8):
                g_copy(mask).wait_recv()
            wide = ghr.shape[2]
            tall = ght.shape[0]
            eye = (
                lax.broadcasted_iota(jnp.int32, (tall, wide), 0)
                == lax.broadcasted_iota(jnp.int32, (tall, wide), 1)
            ).astype(jnp.float32).astype(jnp.bfloat16)
            ght[...] = lax.dot_general(
                eye, ghr[...].reshape(8 * rows, wide), (((1,), (1,)), ((), ())),
                preferred_element_type=jnp.float32,
            ).astype(jnp.bfloat16)
        c = chunk_of(step)

        @pl.loop(0, part.shape[2] // 256)
        def _(tile):
            cols = pl.ds(pl.multiple_of(tile * 256, 256), 256)
            part[c, :, cols] = jnp.dot(
                ght[...], cg[c, :, :, cols].reshape(8 * rows, 256),
                preferred_element_type=jnp.float32,
            )

        @pl.when((z == 0) & (c > 0))
        def _():
            sendbuf[c] = part[c].astype(sendbuf.dtype)
            r_copy(c, True).start()

        @pl.when((z == last) & (c < last))
        def _():
            sendbuf[c] = part[c].astype(sendbuf.dtype)
            r_copy(c, False).start()

        if step < last:
            w_step(step + 1)
        if step == last - 1:

            @pl.when(middle & low)
            def _():
                r_pass(last, True)

            @pl.when(middle & jnp.logical_not(low))
            def _():
                r_pass(0, False)

    @pl.loop(0, 4)
    def _(tile):
        total = None
        for d in range(parts):
            term = lax.dot_general(
                cg[d, pl.ds(tile * 2, 2)].reshape(2 * rows, cg.shape[3]), wfull[d],
                (((1,), (1,)), ((), ())), preferred_element_type=jnp.float32,
            )
            total = term if total is None else total + term
        backs[pl.ds(tile * 2, 2)] = total.astype(jnp.bfloat16).reshape(2, rows, backs.shape[2])

    def b_copy(mask):
        p = peer(mask)
        return remote(backs.at[p], backr_ref.at[e], b_send.at[mask], b_recv.at[mask], (z, p))

    for mask in (6, 2, 4, 7, 3, 5, 1):
        b_copy(mask).start()
    backr_ref[e] = backs[e]

    for i in range(last):
        right, left = last - i, i
        more_right = middle & (z < right)
        more_left = middle & (z > left)
        if i == 0:
            more_right = more_right & jnp.logical_not(low)
            more_left = more_left & low

        @pl.when(more_right)
        def _():
            r_pass(right, True)

        @pl.when(more_left)
        def _():
            r_pass(left, False)

    @pl.when(z > 0)
    def _():
        r_wait(z, True)
        part[z] = part[z] + from_left[z].astype(jnp.float32)

    @pl.when(z < last)
    def _():
        r_wait(z, False)
        part[z] = part[z] + from_right[z].astype(jnp.float32)

    gd_ref[...] = part[z]

    for mask in range(1, 8):
        b_copy(mask).wait_recv()
    for mask in range(1, 8):
        b_copy(mask).wait_send()
        g_copy(mask).wait_send()
    for step in range(parts):
        for copy in copies[step]:
            copy.wait_send()
    for hop in range(last):

        @pl.when((z >= hop) & (z < last))
        def _():
            w_copy(hop, True).wait_send()

        @pl.when((z + hop <= last) & (z > 0))
        def _():
            w_copy(hop, False).wait_send()

    for c in range(parts):

        @pl.when(z < c)
        def _():
            r_copy(c, True).wait_send()

        @pl.when(z > c)
        def _():
            r_copy(c, False).wait_send()


def fused(grad_out, hidden_act, gate_weights, routing, resp_lengths, advantage, w_down):
    rows, width = grad_out.shape
    ffw = hidden_act.shape[2]
    parts = lax.axis_size("dp")
    cols = width // parts
    wide = round_up(cols, 256)
    tall = round_up(ffw, 16)
    lanes = round_up(ffw, 128)
    scale = token_scale(resp_lengths, advantage, rows)
    cotan = (scale[:, None] * grad_out.astype(jnp.float32)).astype(jnp.bfloat16)
    cot = jnp.pad(
        cotan.reshape(rows, parts, cols).transpose(1, 0, 2), ((0, 0), (0, 0), (0, wide - cols))
    )
    gates = gate_weights.astype(jnp.float32)
    hidden = hidden_act.astype(jnp.float32)
    scaled = (gates[:, :, None] * hidden).astype(jnp.bfloat16)
    named = routing[None] == jnp.arange(8, dtype=jnp.int32)[:, None, None]
    gh = jnp.sum(
        jnp.where(named[..., None], scaled[None], jnp.zeros((), jnp.bfloat16)).astype(jnp.float32),
        axis=2,
    ).astype(jnp.bfloat16)
    gh = jnp.pad(gh, ((0, 0), (0, 0), (0, lanes - ffw)))
    w = jnp.pad(w_down[0], ((0, tall - ffw), (0, wide - cols)))
    vmem = pl.BlockSpec(memory_space=pltpu.VMEM)
    dma = pltpu.SemaphoreType.DMA
    bf16, f32 = jnp.bfloat16, jnp.float32
    total, back = pl.pallas_call(
        functools.partial(exchange_kernel, parts),
        out_shape=(
            jax.ShapeDtypeStruct((tall, wide), f32),
            jax.ShapeDtypeStruct((8, rows, tall), bf16),
        ),
        in_specs=[vmem] * 3,
        out_specs=(vmem, vmem),
        scratch_shapes=[
            pltpu.VMEM((parts, 8, rows, wide), bf16),
            pltpu.VMEM((8, rows, lanes), bf16),
            pltpu.VMEM((tall, 8 * rows), bf16),
            pltpu.VMEM((parts, tall, wide), bf16),
            pltpu.VMEM((parts, tall, wide), f32),
            pltpu.VMEM((parts, tall, wide), bf16),
            pltpu.VMEM((parts, tall, wide), bf16),
            pltpu.VMEM((parts, tall, wide), bf16),
            pltpu.VMEM((8, rows, tall), bf16),
            dma((parts, 8)), dma((parts, 8)),
            dma((8,)), dma((8,)),
            dma((2, parts)), dma((2, parts)),
            dma((2, parts)), dma((2, parts)),
            dma((8,)), dma((8,)),
        ],
        compiler_params=pltpu.CompilerParams(
            collective_id=0, has_side_effects=True, vmem_limit_bytes=52 * 1024 * 1024
        ),
        cost_estimate=pl.CostEstimate(
            flops=32 * rows * width * tall, bytes_accessed=8 * rows * width * 2, transcendentals=0
        ),
    )(cot, gh, w)
    grad_down = total[None, :ffw, :cols]
    back = back[:, :, :ffw].astype(f32)
    mine = jnp.sum(jnp.where(named[..., None], back[:, :, None, :], 0.0), axis=0)
    grad_gates = jnp.sum(mine * hidden, axis=2)
    grad_hidden = gates[:, :, None] * mine
    return (grad_down, grad_hidden, grad_gates)


def solution(mesh):
    fits = mesh.shape["expert"] == 8 and 2 <= mesh.shape["dp"] <= 4
    body = fused if fits else local

    placed = (
        P(("dp", "expert"), None),
        P(("dp", "expert"), None, None),
        P(("dp", "expert"), None),
        P(("dp", "expert"), None),
        P(("dp", "expert"), None),
        P(("dp", "expert"), None),
        P("expert", None, "dp"),
    )
    return jax.shard_map(
        body,
        mesh=mesh,
        in_specs=placed,
        out_specs=(
            P("expert", None, "dp"),
            P(("dp", "expert"), None, None),
            P(("dp", "expert"), None),
        ),
        check_vma=False,
    )
```

```python
import functools

import jax
import jax.numpy as jnp
from jax import lax
from jax.experimental import pallas as pl
from jax.experimental.pallas import tpu as pltpu
from jax.sharding import PartitionSpec as P


def weight_terms(hid_recv, gated):
    partial_term = lax.dot_general(
        hid_recv, gated, (((0,), (0,)), ((), ())), preferred_element_type=jnp.float32
    )
    return lax.psum_scatter(partial_term, "dp", scatter_dimension=1, tiled=True)[None]


def local(grad_out, hidden_act, gate_weights, routing, resp_lengths, advantage, w_down):
    rows = grad_out.shape[0]
    width = grad_out.shape[1]
    topk = routing.shape[1]
    ffw = hidden_act.shape[2]
    nexp = lax.axis_size("expert")
    cap = min(rows, 5 * rows * topk // (4 * nexp))
    items = rows * topk
    slots = nexp * cap
    ends = jnp.cumsum(resp_lengths[0])
    starts = ends - resp_lengths[0]
    position = jnp.arange(rows, dtype=jnp.int32)
    inside = (position[:, None] >= starts[None, :]) & (position[:, None] < ends[None, :])
    ratio = advantage[0] / resp_lengths[0].astype(jnp.float32)
    scale = jnp.sum(jnp.where(inside, ratio[None, :], 0.0), axis=1)
    cotan = (scale[:, None] * grad_out.astype(jnp.float32)).astype(jnp.bfloat16)
    dest = routing.reshape(-1)
    onehot = (dest[:, None] == jnp.arange(nexp, dtype=jnp.int32)[None, :]).astype(jnp.int32)
    rank = jnp.cumsum(onehot, axis=0) - onehot
    place = jnp.sum(rank * onehot, axis=1)
    flat = dest * cap + place
    slot_item = (
        jnp.full((slots,), items, jnp.int32).at[flat].set(jnp.arange(items, dtype=jnp.int32))
    )
    valid = slot_item < items
    safe = jnp.minimum(slot_item, items - 1)
    send_cot = jnp.where(valid[:, None], cotan[safe // topk], jnp.zeros((), jnp.bfloat16))
    send_hid = jnp.where(
        valid[:, None], hidden_act.reshape(items, ffw)[safe], jnp.zeros((), jnp.bfloat16)
    )
    send_gate = jnp.where(valid, gate_weights.reshape(items)[safe], jnp.zeros((), jnp.bfloat16))
    recv_cot, recv_hid, recv_gate = (
        lax.all_to_all(
            send_cot.reshape(nexp, cap, width), "expert", split_axis=0, concat_axis=0, tiled=True
        ),
        lax.all_to_all(
            send_hid.reshape(nexp, cap, ffw), "expert", split_axis=0, concat_axis=0, tiled=True
        ),
        lax.all_to_all(
            send_gate.reshape(nexp, cap), "expert", split_axis=0, concat_axis=0, tiled=True
        ),
    )
    recv_cot = recv_cot.reshape(slots, width)
    recv_hid = recv_hid.reshape(slots, ffw)
    recv_gate = recv_gate.reshape(slots).astype(jnp.float32)
    gated = (recv_gate[:, None] * recv_cot.astype(jnp.float32)).astype(jnp.bfloat16)
    local_weight = w_down[0]
    piece = lax.all_gather(local_weight, "dp", axis=1, tiled=True)
    back_sum = lax.dot_general(
        recv_cot, piece, (((1,), (1,)), ((), ())), preferred_element_type=jnp.float32
    )
    output = jnp.dot(recv_hid, piece, preferred_element_type=jnp.float32)
    gate_sum = jnp.sum(recv_cot.astype(jnp.float32) * output, axis=1)
    dhid = recv_gate[:, None] * back_sum
    result_hid, result_gate = (
        lax.all_to_all(
            dhid.reshape(nexp, cap, ffw), "expert", split_axis=0, concat_axis=0, tiled=True
        ),
        lax.all_to_all(
            gate_sum.reshape(nexp, cap), "expert", split_axis=0, concat_axis=0, tiled=True
        ),
    )
    grad_down = weight_terms(recv_hid, gated)
    grad_hidden = result_hid.reshape(slots, ffw)[flat].reshape(rows, topk, ffw)
    grad_gates = result_gate.reshape(slots)[flat].reshape(rows, topk)
    return (grad_down, grad_hidden, grad_gates)


MESH = pl.DeviceIdType.MESH
SIB, ALONG_X, ALONG_Y = 1, 2, 4


def round_up(size, unit):
    return -(-size // unit) * unit


def exchange_kernel(
    parts, len_ref, adv_ref, out_ref, hid_ref, gate_ref, route_ref, w_ref, gd_ref, mine_ref,
    cg, early, gh, backr, ghr, ght, wfull, part, sendbuf, from_left, from_right, backs,
    c_send, c_recv, g_send, g_recv, w_send, w_recv, r_send, r_recv, b_send, b_recv,
):
    z = lax.axis_index("dp")
    e = lax.axis_index("expert")
    core, xpos, ypos = e % 2, (e // 2) % 2, e // 4
    last = parts - 1
    cols, rows = out_ref.shape[1:]
    ffw = hid_ref.shape[1]
    tall = gh.shape[1]
    half = round_up(cols // 2, 16)
    low = 2 * z < parts

    def peer(mask):
        c = 1 - core if mask & 1 else core
        x = 1 - xpos if mask & 2 else xpos
        y = 1 - ypos if mask & 4 else ypos
        return (y * 2 + x) * 2 + c

    barrier = pltpu.get_barrier_semaphore()
    for mask in range(1, 8):
        pl.semaphore_signal(barrier, inc=1, device_id=(z, peer(mask)), device_id_type=MESH)

    @pl.when(z > 0)
    def _():
        pl.semaphore_signal(barrier, inc=1, device_id=(z - 1, e), device_id_type=MESH)

    @pl.when(z < last)
    def _():
        pl.semaphore_signal(barrier, inc=1, device_id=(z + 1, e), device_id_type=MESH)

    wfull[z] = jnp.zeros(wfull.shape[1:], jnp.bfloat16)
    wfull[z, 0:ffw] = w_ref[...]
    routes = route_ref[...]
    gates = gate_ref[...].astype(jnp.float32)
    scaled = [
        (gates[k : k + 1] * hid_ref[k].astype(jnp.float32)).astype(jnp.bfloat16)
        .astype(jnp.float32)
        for k in range(hid_ref.shape[0])
    ]
    for expert in range(8):
        own = jnp.zeros((ffw, rows), jnp.float32)
        for k, block in enumerate(scaled):
            own = jnp.where(routes[k : k + 1] == expert, block, own)
        own = jnp.concatenate([own, jnp.zeros((tall - ffw, rows), jnp.float32)], axis=0)
        gh[expert] = own.astype(jnp.bfloat16)

    position = lax.broadcasted_iota(jnp.int32, (8, rows), 1)
    scale = jnp.zeros((8, rows), jnp.float32)
    start = 0
    for s in range(len_ref.shape[1]):
        length = len_ref[0, s]
        end = start + length
        ratio = jnp.full((8, rows), adv_ref[0, s]) / jnp.full(
            (8, rows), length.astype(jnp.float32)
        )
        scale = scale + jnp.where((position >= start) & (position < end), ratio, 0.0)
        start = end
    scale = scale[0:1]
    for c in range(parts):
        cg[c, e] = (scale * out_ref[c].astype(jnp.float32)).astype(jnp.bfloat16)

    pl.semaphore_wait(barrier, 7 + jnp.minimum(z, 1) + jnp.minimum(last - z, 1))

    def remote(src, dst, send, recv, device):
        return pltpu.make_async_remote_copy(
            src_ref=src, dst_ref=dst, send_sem=send, recv_sem=recv,
            device_id=device, device_id_type=MESH,
        )

    def w_copy(hop, rightward):
        origin = z - hop if rightward else z + hop
        side = 0 if rightward else 1
        src = wfull.at[origin]
        target = z + 1 if rightward else z - 1
        return remote(
            src, wfull.at[origin], w_send.at[side, hop], w_recv.at[side, hop], (target, e)
        )

    def w_recv_wait(hop, rightward):
        origin = z - 1 - hop if rightward else z + 1 + hop
        side = 0 if rightward else 1
        remote(
            wfull.at[origin], wfull.at[origin], w_send.at[side, hop], w_recv.at[side, hop],
            (z, peer(SIB)),
        ).wait_recv()

    def w_step(hop):
        for rightward in (True, False):
            if hop > 0:
                come = z >= hop if rightward else z + hop <= last

                @pl.when(come)
                def _(rightward=rightward):
                    w_recv_wait(hop - 1, rightward)

            if hop < last:
                go = (z >= hop) & (z < last) if rightward else (z + hop <= last) & (z > 0)

                @pl.when(go)
                def _(rightward=rightward):
                    w_copy(hop, rightward).start()

    def g_copy(mask):
        p = peer(mask)
        return remote(gh.at[p], ghr.at[e], g_send.at[mask], g_recv.at[mask], (z, p))

    def chunk_of(step):
        return jnp.where(low, (z + parts - 1 - step) % parts, (z + 1 + step) % parts)

    def c_own(step, kind, mask):
        c = chunk_of(step)
        return remote(
            cg.at[c, e], cg.at[c, e], c_send.at[step, kind], c_recv.at[step, kind],
            (z, peer(mask)),
        )

    def c_pass(step, kind, source, mask, first=None):
        c = chunk_of(step)
        ref = cg.at[c, peer(source)]
        if first is not None:
            count = half if first == 0 else cols - half
            ref = cg.at[c, peer(source), pl.ds(first, count)]
        return remote(
            ref, ref, c_send.at[step, kind], c_recv.at[step, kind], (z, peer(mask))
        )

    def c_copies(step):
        return [
            c_own(step, 0, SIB), c_own(step, 1, ALONG_X), c_own(step, 2, ALONG_Y),
            c_pass(step, 3, ALONG_X, ALONG_Y, 0),
            c_pass(step, 4, ALONG_Y, ALONG_X, half),
            c_pass(step, 5, ALONG_X, SIB), c_pass(step, 6, ALONG_Y, SIB),
            c_pass(step, 7, ALONG_X | ALONG_Y, SIB),
        ]

    copies = [c_copies(step) for step in range(parts)]

    w_step(0)
    for mask in (6, 2, 4, 1, 3, 5, 7):
        g_copy(mask).start()
    for kind in (1, 2, 0):
        copies[0][kind].start()
    ghr[e] = gh[e]

    def gather(step):
        for kind in (1, 2):
            copies[step][kind].wait_recv()
        for kind in (3, 4):
            copies[step][kind].start()
        if step + 1 < parts:
            for kind in (1, 2, 0):
                copies[step + 1][kind].start()
        for kind in (5, 6):
            copies[step][kind].start()
        if step == 0:
            w_step(1)
        for kind in (3, 4):
            copies[step][kind].wait_recv()
        copies[step][7].start()
        for kind in (0, 5, 6, 7):
            copies[step][kind].wait_recv()

    def r_copy(c, rightward):
        side = 0 if rightward else 1
        dst = from_left if rightward else from_right
        return remote(
            sendbuf.at[c], dst.at[c], r_send.at[side, c], r_recv.at[side, c],
            (z + 1 if rightward else z - 1, e),
        )

    def r_wait(c, rightward):
        side = 0 if rightward else 1
        dst = from_left if rightward else from_right
        remote(
            sendbuf.at[c], dst.at[c], r_send.at[side, c], r_recv.at[side, c], (z, peer(SIB))
        ).wait_recv()

    def r_pass(c, rightward):
        r_wait(c, rightward)
        came = (from_left if rightward else from_right)[c].astype(jnp.float32)
        sendbuf[c] = (part[c] + came).astype(sendbuf.dtype)
        r_copy(c, rightward).start()

    middle = (z > 0) & (z < last)

    for step in range(parts):
        gather(step)
        if step == 0:
            for mask in range(1, 8):
                g_copy(mask).wait_recv()
            ght[...] = jnp.concatenate([ghr[p] for p in range(8)], axis=1)
        c = chunk_of(step)

        for first in range(0, cols, 256):
            count = min(256, cols - first)
            block = jnp.concatenate([cg[c, p, first : first + count] for p in range(8)], axis=1)
            part[c, :, first : first + count] = lax.dot_general(
                ght[...], block, (((1,), (1,)), ((), ())), preferred_element_type=jnp.float32
            )

        @pl.when((z == 0) & (c > 0))
        def _():
            sendbuf[c] = part[c].astype(sendbuf.dtype)
            r_copy(c, True).start()

        @pl.when((z == last) & (c < last))
        def _():
            sendbuf[c] = part[c].astype(sendbuf.dtype)
            r_copy(c, False).start()

        if 2 <= step < last:
            w_step(step)
        if step == last - 1:

            @pl.when(middle & low)
            def _():
                r_pass(last, True)

            @pl.when(middle & jnp.logical_not(low))
            def _():
                r_pass(0, False)

    far = jnp.where(low, last, 0)

    def back_term(tile, d):
        pair = jnp.concatenate([cg[d, 2 * tile], cg[d, 2 * tile + 1]], axis=1)
        return jnp.dot(wfull[d], pair, preferred_element_type=jnp.float32)

    def b_copy(mask):
        p = peer(mask)
        return remote(backs.at[p], backr.at[e], b_send.at[mask], b_recv.at[mask], (z, p))

    @pl.loop(0, 4)
    def _(tile):
        total = back_term(tile, (far + 1) % parts)
        for i in range(2, parts):
            total = total + back_term(tile, (far + i) % parts)
        early[tile] = total

    if last > 1:
        w_step(last)
    for mask in (ALONG_X | ALONG_Y, ALONG_X, ALONG_Y, 0):
        tile = peer(mask) // 2
        total = early[tile] + back_term(tile, far)
        total = total.astype(jnp.bfloat16)
        backs[2 * tile] = total[:, :rows]
        backs[2 * tile + 1] = total[:, rows:]
        if mask:
            b_copy(mask).start()
        b_copy(mask | SIB).start()
    backr[e] = backs[e]

    for i in range(last):
        right, left = last - i, i
        more_right = middle & (z < right)
        more_left = middle & (z > left)
        if i == 0:
            more_right = more_right & jnp.logical_not(low)
            more_left = more_left & low

        @pl.when(more_right)
        def _():
            r_pass(right, True)

        @pl.when(more_left)
        def _():
            r_pass(left, False)

    for mask in range(1, 8):
        b_copy(mask).wait_recv()
    for k in range(mine_ref.shape[0]):
        mine = jnp.zeros((tall, rows), jnp.float32)
        for expert in range(8):
            mine = jnp.where(routes[k : k + 1] == expert, backr[expert].astype(jnp.float32), mine)
        mine_ref[k] = mine.astype(jnp.bfloat16)

    @pl.when(z > 0)
    def _():
        r_wait(z, True)
        part[z] = part[z] + from_left[z].astype(jnp.float32)

    @pl.when(z < last)
    def _():
        r_wait(z, False)
        part[z] = part[z] + from_right[z].astype(jnp.float32)

    gd_ref[...] = part[z][:ffw]

    for mask in range(1, 8):
        b_copy(mask).wait_send()
        g_copy(mask).wait_send()
    for step in range(parts):
        for copy in copies[step]:
            copy.wait_send()
    for hop in range(last):

        @pl.when((z >= hop) & (z < last))
        def _():
            w_copy(hop, True).wait_send()

        @pl.when((z + hop <= last) & (z > 0))
        def _():
            w_copy(hop, False).wait_send()

    for c in range(parts):

        @pl.when(z < c)
        def _():
            r_copy(c, True).wait_send()

        @pl.when(z > c)
        def _():
            r_copy(c, False).wait_send()


def fused(grad_out, hidden_act, gate_weights, routing, resp_lengths, advantage, w_down):
    rows, width = grad_out.shape
    ffw = hidden_act.shape[2]
    parts = lax.axis_size("dp")
    cols = width // parts
    tall = round_up(ffw, 16)
    topk = routing.shape[1]
    vmem = pl.BlockSpec(memory_space=pltpu.VMEM)
    smem = pl.BlockSpec(memory_space=pltpu.SMEM)
    dma = pltpu.SemaphoreType.DMA
    bf16, f32 = jnp.bfloat16, jnp.float32
    total, mine = pl.pallas_call(
        functools.partial(exchange_kernel, parts),
        out_shape=(
            jax.ShapeDtypeStruct((ffw, cols), f32),
            jax.ShapeDtypeStruct((topk, tall, rows), bf16),
        ),
        in_specs=[smem] * 2 + [vmem] * 5,
        out_specs=(vmem, vmem),
        scratch_shapes=[
            pltpu.VMEM((parts, 8, cols, rows), bf16),
            pltpu.VMEM((4, tall, 2 * rows), f32),
            pltpu.VMEM((8, tall, rows), bf16),
            pltpu.VMEM((8, tall, rows), bf16),
            pltpu.VMEM((8, tall, rows), bf16),
            pltpu.VMEM((tall, 8 * rows), bf16),
            pltpu.VMEM((parts, tall, cols), bf16),
            pltpu.VMEM((parts, tall, cols), f32),
            pltpu.VMEM((parts, tall, cols), bf16),
            pltpu.VMEM((parts, tall, cols), bf16),
            pltpu.VMEM((parts, tall, cols), bf16),
            pltpu.VMEM((8, tall, rows), bf16),
            dma((parts, 8)), dma((parts, 8)),
            dma((8,)), dma((8,)),
            dma((2, parts)), dma((2, parts)),
            dma((2, parts)), dma((2, parts)),
            dma((8,)), dma((8,)),
        ],
        compiler_params=pltpu.CompilerParams(
            collective_id=0, has_side_effects=True, vmem_limit_bytes=52 * 1024 * 1024
        ),
        cost_estimate=pl.CostEstimate(
            flops=32 * rows * width * tall, bytes_accessed=8 * rows * width * 2, transcendentals=0
        ),
    )(
        resp_lengths, advantage, grad_out.T.reshape(parts, cols, rows),
        hidden_act.transpose(1, 2, 0), gate_weights.T, routing.T, w_down[0],
    )
    mine = mine[:, :ffw].astype(f32).transpose(2, 0, 1)
    grad_down = total[None]
    grad_gates = jnp.sum(mine * hidden_act.astype(f32), axis=2)
    grad_hidden = gate_weights.astype(f32)[:, :, None] * mine
    return (grad_down, grad_hidden, grad_gates)


def solution(mesh):
    fits = mesh.shape["expert"] == 8 and mesh.shape["dp"] in (2, 4)
    body = fused if fits else local

    placed = (
        P(("dp", "expert"), None),
        P(("dp", "expert"), None, None),
        P(("dp", "expert"), None),
        P(("dp", "expert"), None),
        P(("dp", "expert"), None),
        P(("dp", "expert"), None),
        P("expert", None, "dp"),
    )
    return jax.shard_map(
        body,
        mesh=mesh,
        in_specs=placed,
        out_specs=(
            P("expert", None, "dp"),
            P(("dp", "expert"), None, None),
            P(("dp", "expert"), None),
        ),
        check_vma=False,
    )
```

```python
import functools

import jax
import jax.numpy as jnp
from jax import lax
from jax.experimental import pallas as pl
from jax.experimental.pallas import tpu as pltpu
from jax.sharding import PartitionSpec as P


def weight_terms(hid_recv, gated):
    partial_term = lax.dot_general(
        hid_recv, gated, (((0,), (0,)), ((), ())), preferred_element_type=jnp.float32
    )
    return lax.psum_scatter(partial_term, "dp", scatter_dimension=1, tiled=True)[None]


def local(grad_out, hidden_act, gate_weights, routing, resp_lengths, advantage, w_down):
    rows = grad_out.shape[0]
    width = grad_out.shape[1]
    topk = routing.shape[1]
    ffw = hidden_act.shape[2]
    nexp = lax.axis_size("expert")
    cap = min(rows, 5 * rows * topk // (4 * nexp))
    items = rows * topk
    slots = nexp * cap
    ends = jnp.cumsum(resp_lengths[0])
    starts = ends - resp_lengths[0]
    position = jnp.arange(rows, dtype=jnp.int32)
    inside = (position[:, None] >= starts[None, :]) & (position[:, None] < ends[None, :])
    ratio = advantage[0] / resp_lengths[0].astype(jnp.float32)
    scale = jnp.sum(jnp.where(inside, ratio[None, :], 0.0), axis=1)
    cotan = (scale[:, None] * grad_out.astype(jnp.float32)).astype(jnp.bfloat16)
    dest = routing.reshape(-1)
    onehot = (dest[:, None] == jnp.arange(nexp, dtype=jnp.int32)[None, :]).astype(jnp.int32)
    rank = jnp.cumsum(onehot, axis=0) - onehot
    place = jnp.sum(rank * onehot, axis=1)
    flat = dest * cap + place
    slot_item = (
        jnp.full((slots,), items, jnp.int32).at[flat].set(jnp.arange(items, dtype=jnp.int32))
    )
    valid = slot_item < items
    safe = jnp.minimum(slot_item, items - 1)
    send_cot = jnp.where(valid[:, None], cotan[safe // topk], jnp.zeros((), jnp.bfloat16))
    send_hid = jnp.where(
        valid[:, None], hidden_act.reshape(items, ffw)[safe], jnp.zeros((), jnp.bfloat16)
    )
    send_gate = jnp.where(valid, gate_weights.reshape(items)[safe], jnp.zeros((), jnp.bfloat16))
    recv_cot, recv_hid, recv_gate = (
        lax.all_to_all(
            send_cot.reshape(nexp, cap, width), "expert", split_axis=0, concat_axis=0, tiled=True
        ),
        lax.all_to_all(
            send_hid.reshape(nexp, cap, ffw), "expert", split_axis=0, concat_axis=0, tiled=True
        ),
        lax.all_to_all(
            send_gate.reshape(nexp, cap), "expert", split_axis=0, concat_axis=0, tiled=True
        ),
    )
    recv_cot = recv_cot.reshape(slots, width)
    recv_hid = recv_hid.reshape(slots, ffw)
    recv_gate = recv_gate.reshape(slots).astype(jnp.float32)
    gated = (recv_gate[:, None] * recv_cot.astype(jnp.float32)).astype(jnp.bfloat16)
    local_weight = w_down[0]
    piece = lax.all_gather(local_weight, "dp", axis=1, tiled=True)
    back_sum = lax.dot_general(
        recv_cot, piece, (((1,), (1,)), ((), ())), preferred_element_type=jnp.float32
    )
    output = jnp.dot(recv_hid, piece, preferred_element_type=jnp.float32)
    gate_sum = jnp.sum(recv_cot.astype(jnp.float32) * output, axis=1)
    dhid = recv_gate[:, None] * back_sum
    result_hid, result_gate = (
        lax.all_to_all(
            dhid.reshape(nexp, cap, ffw), "expert", split_axis=0, concat_axis=0, tiled=True
        ),
        lax.all_to_all(
            gate_sum.reshape(nexp, cap), "expert", split_axis=0, concat_axis=0, tiled=True
        ),
    )
    grad_down = weight_terms(recv_hid, gated)
    grad_hidden = result_hid.reshape(slots, ffw)[flat].reshape(rows, topk, ffw)
    grad_gates = result_gate.reshape(slots)[flat].reshape(rows, topk)
    return (grad_down, grad_hidden, grad_gates)


MESH = pl.DeviceIdType.MESH
SIB, ALONG_X, ALONG_Y = 1, 2, 4


def round_up(size, unit):
    return -(-size // unit) * unit


def exchange_kernel(
    parts, len_hbm, adv_hbm, out_hbm, hid_hbm, gate_hbm, route_hbm, w_hbm, gd_ref, mine_ref,
    len_ref, adv_ref, out_ref, hid_ref, gate_ref, route_ref, w_ref,
    cg, early, gh, backr, ghr, ght, wfull, part, sendbuf, from_left, from_right, backs,
    c_send, c_recv, g_send, g_recv, w_send, w_recv, r_send, r_recv, b_send, b_recv, in_sem,
):
    z = lax.axis_index("dp")
    e = lax.axis_index("expert")
    core, xpos, ypos = e % 2, (e // 2) % 2, e // 4
    last = parts - 1
    cols, rows = out_ref.shape[1:]
    ffw = hid_ref.shape[1]
    tall = gh.shape[1]
    split = min(cols, round_up(cols // 2, 128))
    spans = ((0, split), (split, cols - split))
    lanes = (pl.ds(0, split), pl.ds(split, part.shape[2] - split))
    w_half = round_up(tall // 2, 16)
    w_rows = (pl.ds(0, w_half), pl.ds(w_half, tall - w_half))
    units = 2 * parts
    loads = [
        pltpu.make_async_copy(src, dst, in_sem.at[i])
        for i, (src, dst) in enumerate((
            (w_hbm, w_ref), (route_hbm, route_ref), (gate_hbm, gate_ref), (hid_hbm, hid_ref),
            (len_hbm, len_ref), (adv_hbm, adv_ref), (out_hbm, out_ref),
        ))
    ]
    for load in loads:
        load.start()
    low = 2 * z < parts

    def peer(mask):
        c = 1 - core if mask & 1 else core
        x = 1 - xpos if mask & 2 else xpos
        y = 1 - ypos if mask & 4 else ypos
        return (y * 2 + x) * 2 + c

    barrier = pltpu.get_barrier_semaphore()
    for mask in range(1, 8):
        pl.semaphore_signal(barrier, inc=1, device_id=(z, peer(mask)), device_id_type=MESH)

    @pl.when(z > 0)
    def _():
        pl.semaphore_signal(barrier, inc=1, device_id=(z - 1, e), device_id_type=MESH)

    @pl.when(z < last)
    def _():
        pl.semaphore_signal(barrier, inc=1, device_id=(z + 1, e), device_id_type=MESH)

    wfull[z] = jnp.zeros(wfull.shape[1:], jnp.bfloat16)
    loads[0].wait()
    wfull[z, 0:ffw, 0:cols] = w_ref[...]
    pl.semaphore_wait(barrier, 7 + jnp.minimum(z, 1) + jnp.minimum(last - z, 1))

    def remote(src, dst, send, recv, device):
        return pltpu.make_async_remote_copy(
            src_ref=src, dst_ref=dst, send_sem=send, recv_sem=recv,
            device_id=device, device_id_type=MESH,
        )

    def w_copy(hop, h, rightward):
        origin = z - hop if rightward else z + hop
        side = 0 if rightward else 1
        target = z + 1 if rightward else z - 1
        ref = wfull.at[origin, w_rows[h]]
        return remote(
            ref, ref, w_send.at[side, hop, h], w_recv.at[side, hop, h], (target, e)
        )

    def w_recv_wait(hop, h, rightward):
        origin = z - 1 - hop if rightward else z + 1 + hop
        side = 0 if rightward else 1
        ref = wfull.at[origin, w_rows[h]]
        remote(
            ref, ref, w_send.at[side, hop, h], w_recv.at[side, hop, h], (z, peer(SIB))
        ).wait_recv()

    def w_step(hop, h):
        for rightward in (True, False):
            if hop > 0:
                come = z >= hop if rightward else z + hop <= last

                @pl.when(come)
                def _(rightward=rightward):
                    w_recv_wait(hop - 1, h, rightward)

            if hop < last:
                go = (z >= hop) & (z < last) if rightward else (z + hop <= last) & (z > 0)

                @pl.when(go)
                def _(rightward=rightward):
                    w_copy(hop, h, rightward).start()

    def g_copy(mask):
        p = peer(mask)
        return remote(gh.at[p], ghr.at[e], g_send.at[mask], g_recv.at[mask], (z, p))

    def chunk_of(step):
        return jnp.where(low, (z + parts - 1 - step) % parts, (z + 1 + step) % parts)

    def c_copy(unit, kind, source, mask, part_of=None):
        c, (first, count) = chunk_of(unit // 2), spans[unit % 2]
        if part_of is not None:
            near = round_up(count // 2, 16)
            first, count = (first, near) if part_of == 0 else (first + near, count - near)
        ref = cg.at[c, peer(source), pl.ds(first, count)]
        return remote(
            ref, ref, c_send.at[unit, kind], c_recv.at[unit, kind], (z, peer(mask))
        )

    def c_copies(unit):
        return [
            c_copy(unit, 0, 0, SIB), c_copy(unit, 1, 0, ALONG_X), c_copy(unit, 2, 0, ALONG_Y),
            c_copy(unit, 3, ALONG_X, ALONG_Y, 0), c_copy(unit, 4, ALONG_Y, ALONG_X, 1),
            c_copy(unit, 5, ALONG_X, SIB), c_copy(unit, 6, ALONG_Y, SIB),
            c_copy(unit, 7, ALONG_X | ALONG_Y, SIB),
        ]

    copies = [c_copies(unit) for unit in range(units)]

    w_step(0, 0)
    w_step(0, 1)

    for load in loads[1:4]:
        load.wait()
    routes = route_ref[...]
    gates = gate_ref[...].astype(jnp.float32)
    scaled = [
        (gates[k : k + 1] * hid_ref[k].astype(jnp.float32)).astype(jnp.bfloat16)
        .astype(jnp.float32)
        for k in range(hid_ref.shape[0])
    ]
    for expert in range(8):
        own = jnp.zeros((ffw, rows), jnp.float32)
        for k, block in enumerate(scaled):
            own = jnp.where(routes[k : k + 1] == expert, block, own)
        own = jnp.concatenate([own, jnp.zeros((tall - ffw, rows), jnp.float32)], axis=0)
        gh[expert] = own.astype(jnp.bfloat16)

    for mask in (6, 2, 4, 1, 3, 5, 7):
        g_copy(mask).start()
    ghr[e] = gh[e]

    for load in loads[4:]:
        load.wait()
    position = lax.broadcasted_iota(jnp.int32, (8, rows), 1)
    scale = jnp.zeros((8, rows), jnp.float32)
    start = 0
    for s in range(len_ref.shape[1]):
        length = len_ref[0, s]
        end = start + length
        ratio = jnp.full((8, rows), adv_ref[0, s]) / jnp.full(
            (8, rows), length.astype(jnp.float32)
        )
        scale = scale + jnp.where((position >= start) & (position < end), ratio, 0.0)
        start = end
    scale = scale[0:1]

    def scale_chunk(step):
        c = chunk_of(step)
        cg[c, e] = (scale * out_ref[c].astype(jnp.float32)).astype(jnp.bfloat16)

    scale_chunk(0)
    for kind in (1, 2, 0):
        copies[0][kind].start()
    for step in range(1, parts):
        scale_chunk(step)

    def gather(unit):
        for kind in (1, 2):
            copies[unit][kind].wait_recv()
        for kind in (3, 4):
            copies[unit][kind].start()
        for later in ((1, 2) if unit == 0 else (unit + 2,)):
            if later < units:
                for kind in (1, 2, 0):
                    copies[later][kind].start()
        for kind in (5, 6):
            copies[unit][kind].start()
        if unit == 0:
            w_step(1, 1)
        for kind in (3, 4):
            copies[unit][kind].wait_recv()
        copies[unit][7].start()
        for kind in (0, 5, 6, 7):
            copies[unit][kind].wait_recv()

    def r_copy(c, h, rightward):
        side = 0 if rightward else 1
        dst = from_left if rightward else from_right
        return remote(
            sendbuf.at[c, :, lanes[h]], dst.at[c, :, lanes[h]],
            r_send.at[side, c, h], r_recv.at[side, c, h],
            (z + 1 if rightward else z - 1, e),
        )

    def r_wait(c, h, rightward):
        side = 0 if rightward else 1
        dst = from_left if rightward else from_right
        remote(
            sendbuf.at[c, :, lanes[h]], dst.at[c, :, lanes[h]],
            r_send.at[side, c, h], r_recv.at[side, c, h], (z, peer(SIB)),
        ).wait_recv()

    def r_pass(c, h, rightward):
        r_wait(c, h, rightward)
        came = (from_left if rightward else from_right)[c, :, lanes[h]].astype(jnp.float32)
        sendbuf[c, :, lanes[h]] = (part[c, :, lanes[h]] + came).astype(sendbuf.dtype)
        r_copy(c, h, rightward).start()

    def r_first(c, h, rightward):
        sendbuf[c, :, lanes[h]] = part[c, :, lanes[h]].astype(sendbuf.dtype)
        r_copy(c, h, rightward).start()

    middle = (z > 0) & (z < last)

    def r_farthest(h, near):
        @pl.when(middle & (low if near else jnp.logical_not(low)))
        def _():
            r_pass(last, h, True)

        @pl.when(middle & (jnp.logical_not(low) if near else low))
        def _():
            r_pass(0, h, False)

    w_step(1, 0)
    for unit in range(units):
        gather(unit)
        h = unit % 2
        if unit == 0:
            for mask in range(1, 8):
                g_copy(mask).wait_recv()
            ght[...] = jnp.concatenate([ghr[p] for p in range(8)], axis=1)
        c = chunk_of(unit // 2)
        first, count = spans[h]
        block = jnp.concatenate([cg[c, p, first : first + count] for p in range(8)], axis=1)
        part[c, :, first : first + count] = lax.dot_general(
            ght[...], block, (((1,), (1,)), ((), ())), preferred_element_type=jnp.float32
        )

        @pl.when((z == 0) & (c > 0))
        def _():
            r_first(c, h, True)

        @pl.when((z == last) & (c < last))
        def _():
            r_first(c, h, False)

        if last > 2:
            if unit == 3:
                w_step(2, 0)
                r_farthest(0, True)
            if unit == 4:
                w_step(2, 1)
            if unit == 5:
                r_farthest(1, True)

    def r_rest(h):
        for i in range(1, last):
            right, left = last - i, i

            @pl.when(middle & (z < right))
            def _(right=right):
                r_pass(right, h, True)

            @pl.when(middle & (z > left))
            def _(left=left):
                r_pass(left, h, False)

    if last > 2:
        r_farthest(0, False)
        r_rest(0)

    far = jnp.where(low, last, 0)

    def back_term(tile, d):
        pair = jnp.concatenate([cg[d, 2 * tile], cg[d, 2 * tile + 1]], axis=1)
        return jnp.dot(wfull[d][:, :cols], pair, preferred_element_type=jnp.float32)

    def b_copy(mask):
        p = peer(mask)
        return remote(backs.at[p], backr.at[e], b_send.at[mask], b_recv.at[mask], (z, p))

    @pl.loop(0, 4)
    def _(tile):
        total = back_term(tile, (far + 1) % parts)
        for i in range(2, parts):
            total = total + back_term(tile, (far + i) % parts)
        early[tile] = total

    if last > 1:
        w_step(last, 0)
        w_step(last, 1)
    for mask in (ALONG_X | ALONG_Y, ALONG_X, ALONG_Y, 0):
        tile = peer(mask) // 2
        total = early[tile] + back_term(tile, far)
        total = total.astype(jnp.bfloat16)
        backs[2 * tile] = total[:, :rows]
        backs[2 * tile + 1] = total[:, rows:]
        if mask:
            b_copy(mask).start()
        b_copy(mask | SIB).start()
    backr[e] = backs[e]

    if last > 2:
        r_farthest(1, False)
        r_rest(1)

    for mask in range(1, 8):
        b_copy(mask).wait_recv()
    for k in range(mine_ref.shape[0]):
        mine = jnp.zeros((tall, rows), jnp.float32)
        for expert in range(8):
            mine = jnp.where(routes[k : k + 1] == expert, backr[expert].astype(jnp.float32), mine)
        mine_ref[k] = mine.astype(jnp.bfloat16)

    for h, (first, count) in enumerate(spans):

        @pl.when(z > 0)
        def _(h=h):
            r_wait(z, h, True)
            part[z, :, lanes[h]] += from_left[z, :, lanes[h]].astype(jnp.float32)

        @pl.when(z < last)
        def _(h=h):
            r_wait(z, h, False)
            part[z, :, lanes[h]] += from_right[z, :, lanes[h]].astype(jnp.float32)

        gd_ref[:, first : first + count] = part[z, 0:ffw, first : first + count]

    for mask in range(1, 8):
        b_copy(mask).wait_send()
        g_copy(mask).wait_send()
    for unit in range(units):
        for copy in copies[unit]:
            copy.wait_send()
    for h in range(2):
        for hop in range(last):

            @pl.when((z >= hop) & (z < last))
            def _():
                w_copy(hop, h, True).wait_send()

            @pl.when((z + hop <= last) & (z > 0))
            def _():
                w_copy(hop, h, False).wait_send()

        for c in range(parts):

            @pl.when(z < c)
            def _():
                r_copy(c, h, True).wait_send()

            @pl.when(z > c)
            def _():
                r_copy(c, h, False).wait_send()


def fused(grad_out, hidden_act, gate_weights, routing, resp_lengths, advantage, w_down):
    rows, width = grad_out.shape
    ffw = hidden_act.shape[2]
    parts = lax.axis_size("dp")
    cols = width // parts
    tall = round_up(ffw, 16)
    topk = routing.shape[1]
    wide = round_up(cols, 128)
    responses = resp_lengths.shape
    vmem = pl.BlockSpec(memory_space=pltpu.VMEM)
    hbm = pl.BlockSpec(memory_space=pl.ANY)
    dma = pltpu.SemaphoreType.DMA
    bf16, f32 = jnp.bfloat16, jnp.float32
    total, mine = pl.pallas_call(
        functools.partial(exchange_kernel, parts),
        out_shape=(
            jax.ShapeDtypeStruct((ffw, cols), f32),
            jax.ShapeDtypeStruct((topk, tall, rows), bf16),
        ),
        in_specs=[hbm] * 7,
        out_specs=(vmem, vmem),
        scratch_shapes=[
            pltpu.SMEM(responses, jnp.int32),
            pltpu.SMEM(responses, f32),
            pltpu.VMEM((parts, cols, rows), bf16),
            pltpu.VMEM((topk, ffw, rows), bf16),
            pltpu.VMEM((topk, rows), bf16),
            pltpu.VMEM((topk, rows), jnp.int32),
            pltpu.VMEM((ffw, cols), bf16),
            pltpu.VMEM((parts, 8, cols, rows), bf16),
            pltpu.VMEM((4, tall, 2 * rows), f32),
            pltpu.VMEM((8, tall, rows), bf16),
            pltpu.VMEM((8, tall, rows), bf16),
            pltpu.VMEM((8, tall, rows), bf16),
            pltpu.VMEM((tall, 8 * rows), bf16),
            pltpu.VMEM((parts, tall, wide), bf16),
            pltpu.VMEM((parts, tall, wide), f32),
            pltpu.VMEM((parts, tall, wide), bf16),
            pltpu.VMEM((parts, tall, wide), bf16),
            pltpu.VMEM((parts, tall, wide), bf16),
            pltpu.VMEM((8, tall, rows), bf16),
            dma((2 * parts, 8)), dma((2 * parts, 8)),
            dma((8,)), dma((8,)),
            dma((2, parts, 2)), dma((2, parts, 2)),
            dma((2, parts, 2)), dma((2, parts, 2)),
            dma((8,)), dma((8,)),
            dma((7,)),
        ],
        compiler_params=pltpu.CompilerParams(
            collective_id=0, has_side_effects=True, vmem_limit_bytes=56 * 1024 * 1024
        ),
        cost_estimate=pl.CostEstimate(
            flops=32 * rows * width * tall, bytes_accessed=8 * rows * width * 2, transcendentals=0
        ),
    )(
        resp_lengths, advantage, grad_out.T.reshape(parts, cols, rows),
        hidden_act.transpose(1, 2, 0), gate_weights.T, routing.T, w_down[0],
    )
    mine = mine[:, :ffw].astype(f32).transpose(2, 0, 1)
    grad_down = total[None]
    grad_gates = jnp.sum(mine * hidden_act.astype(f32), axis=2)
    grad_hidden = gate_weights.astype(f32)[:, :, None] * mine
    return (grad_down, grad_hidden, grad_gates)


def solution(mesh):
    fits = mesh.shape["expert"] == 8 and mesh.shape["dp"] == 4
    body = fused if fits else local

    placed = (
        P(("dp", "expert"), None),
        P(("dp", "expert"), None, None),
        P(("dp", "expert"), None),
        P(("dp", "expert"), None),
        P(("dp", "expert"), None),
        P(("dp", "expert"), None),
        P("expert", None, "dp"),
    )
    return jax.shard_map(
        body,
        mesh=mesh,
        in_specs=placed,
        out_specs=(
            P("expert", None, "dp"),
            P(("dp", "expert"), None, None),
            P(("dp", "expert"), None),
        ),
        check_vma=False,
    )
```

```python
import functools

import jax
import jax.numpy as jnp
from jax import lax
from jax.experimental import pallas as pl
from jax.experimental.pallas import tpu as pltpu
from jax.sharding import PartitionSpec as P


def weight_terms(hid_recv, gated):
    partial_term = lax.dot_general(
        hid_recv, gated, (((0,), (0,)), ((), ())), preferred_element_type=jnp.float32
    )
    return lax.psum_scatter(partial_term, "dp", scatter_dimension=1, tiled=True)[None]


def local(grad_out, hidden_act, gate_weights, routing, resp_lengths, advantage, w_down):
    rows = grad_out.shape[0]
    width = grad_out.shape[1]
    topk = routing.shape[1]
    ffw = hidden_act.shape[2]
    nexp = lax.axis_size("expert")
    cap = min(rows, 5 * rows * topk // (4 * nexp))
    items = rows * topk
    slots = nexp * cap
    ends = jnp.cumsum(resp_lengths[0])
    starts = ends - resp_lengths[0]
    position = jnp.arange(rows, dtype=jnp.int32)
    inside = (position[:, None] >= starts[None, :]) & (position[:, None] < ends[None, :])
    ratio = advantage[0] / resp_lengths[0].astype(jnp.float32)
    scale = jnp.sum(jnp.where(inside, ratio[None, :], 0.0), axis=1)
    cotan = (scale[:, None] * grad_out.astype(jnp.float32)).astype(jnp.bfloat16)
    dest = routing.reshape(-1)
    onehot = (dest[:, None] == jnp.arange(nexp, dtype=jnp.int32)[None, :]).astype(jnp.int32)
    rank = jnp.cumsum(onehot, axis=0) - onehot
    place = jnp.sum(rank * onehot, axis=1)
    flat = dest * cap + place
    slot_item = (
        jnp.full((slots,), items, jnp.int32).at[flat].set(jnp.arange(items, dtype=jnp.int32))
    )
    valid = slot_item < items
    safe = jnp.minimum(slot_item, items - 1)
    send_cot = jnp.where(valid[:, None], cotan[safe // topk], jnp.zeros((), jnp.bfloat16))
    send_hid = jnp.where(
        valid[:, None], hidden_act.reshape(items, ffw)[safe], jnp.zeros((), jnp.bfloat16)
    )
    send_gate = jnp.where(valid, gate_weights.reshape(items)[safe], jnp.zeros((), jnp.bfloat16))
    recv_cot, recv_hid, recv_gate = (
        lax.all_to_all(
            send_cot.reshape(nexp, cap, width), "expert", split_axis=0, concat_axis=0, tiled=True
        ),
        lax.all_to_all(
            send_hid.reshape(nexp, cap, ffw), "expert", split_axis=0, concat_axis=0, tiled=True
        ),
        lax.all_to_all(
            send_gate.reshape(nexp, cap), "expert", split_axis=0, concat_axis=0, tiled=True
        ),
    )
    recv_cot = recv_cot.reshape(slots, width)
    recv_hid = recv_hid.reshape(slots, ffw)
    recv_gate = recv_gate.reshape(slots).astype(jnp.float32)
    gated = (recv_gate[:, None] * recv_cot.astype(jnp.float32)).astype(jnp.bfloat16)
    local_weight = w_down[0]
    piece = lax.all_gather(local_weight, "dp", axis=1, tiled=True)
    back_sum = lax.dot_general(
        recv_cot, piece, (((1,), (1,)), ((), ())), preferred_element_type=jnp.float32
    )
    output = jnp.dot(recv_hid, piece, preferred_element_type=jnp.float32)
    gate_sum = jnp.sum(recv_cot.astype(jnp.float32) * output, axis=1)
    dhid = recv_gate[:, None] * back_sum
    result_hid, result_gate = (
        lax.all_to_all(
            dhid.reshape(nexp, cap, ffw), "expert", split_axis=0, concat_axis=0, tiled=True
        ),
        lax.all_to_all(
            gate_sum.reshape(nexp, cap), "expert", split_axis=0, concat_axis=0, tiled=True
        ),
    )
    grad_down = weight_terms(recv_hid, gated)
    grad_hidden = result_hid.reshape(slots, ffw)[flat].reshape(rows, topk, ffw)
    grad_gates = result_gate.reshape(slots)[flat].reshape(rows, topk)
    return (grad_down, grad_hidden, grad_gates)


MESH = pl.DeviceIdType.MESH
SIB, ALONG_X, ALONG_Y = 1, 2, 4


def round_up(size, unit):
    return -(-size // unit) * unit


def exchange_kernel(
    parts, len_hbm, adv_hbm, out_hbm, hid_hbm, gate_hbm, route_hbm, w_hbm, gd_ref, mine_ref,
    len_ref, adv_ref, out_ref, hid_ref, gate_ref, route_ref, w_ref,
    cg, early, gh, backr, ghr, ght, wfull, part, sendbuf, from_left, from_right, backs,
    wtail, tailpart, tailsend, tail_left, tail_right, turned,
    c_send, c_recv, g_send, g_recv, w_send, w_recv, r_send, r_recv, b_send, b_recv, in_sem,
):
    z = lax.axis_index("dp")
    e = lax.axis_index("expert")
    core, xpos, ypos = e % 2, (e // 2) % 2, e // 4
    last = parts - 1
    cols, rows = out_ref.shape[1:]
    ffw = hid_ref.shape[1]
    tall = gh.shape[1]
    split = min(cols, round_up(cols // 2, 128))
    spans = ((0, split), (split, cols - split))
    main = wfull.shape[2]
    tail = cols - main
    lanes = (pl.ds(0, split), pl.ds(split, main - split))
    w_half = round_up((tall * main + tail * tall) // (2 * main), 16)
    w_rows = (pl.ds(0, w_half), pl.ds(w_half, tall - w_half))
    pieces = ((0,), (1, 2))
    units = 2 * parts
    loads = [
        pltpu.make_async_copy(src, dst, in_sem.at[i])
        for i, (src, dst) in enumerate((
            (w_hbm, w_ref), (route_hbm, route_ref), (gate_hbm, gate_ref), (hid_hbm, hid_ref),
            (len_hbm, len_ref), (adv_hbm, adv_ref), (out_hbm, out_ref),
        ))
    ]
    for load in loads:
        load.start()
    low = 2 * z < parts

    def peer(mask):
        c = 1 - core if mask & 1 else core
        x = 1 - xpos if mask & 2 else xpos
        y = 1 - ypos if mask & 4 else ypos
        return (y * 2 + x) * 2 + c

    barrier = pltpu.get_barrier_semaphore()
    for mask in range(1, 8):
        pl.semaphore_signal(barrier, inc=1, device_id=(z, peer(mask)), device_id_type=MESH)

    @pl.when(z > 0)
    def _():
        pl.semaphore_signal(barrier, inc=1, device_id=(z - 1, e), device_id_type=MESH)

    @pl.when(z < last)
    def _():
        pl.semaphore_signal(barrier, inc=1, device_id=(z + 1, e), device_id_type=MESH)

    loads[0].wait()
    own_w = jnp.concatenate([w_ref[...], jnp.zeros((tall - ffw, cols), jnp.bfloat16)], axis=0)
    wfull[z] = own_w[:, :main]
    chosen = (
        lax.broadcasted_iota(jnp.int32, (tail, cols), 0) + main
        == lax.broadcasted_iota(jnp.int32, (tail, cols), 1)
    ).astype(jnp.float32).astype(jnp.bfloat16)
    wtail[z] = lax.dot_general(
        chosen, own_w, (((1,), (1,)), ((), ())), preferred_element_type=jnp.float32
    ).astype(jnp.bfloat16)
    eye = (
        lax.broadcasted_iota(jnp.int32, (tall, tall), 0)
        == lax.broadcasted_iota(jnp.int32, (tall, tall), 1)
    ).astype(jnp.float32).astype(jnp.bfloat16)

    def turn(block):
        return lax.dot_general(
            eye, block, (((1,), (1,)), ((), ())), preferred_element_type=jnp.float32
        )

    pl.semaphore_wait(barrier, 7 + jnp.minimum(z, 1) + jnp.minimum(last - z, 1))

    def remote(src, dst, send, recv, device):
        return pltpu.make_async_remote_copy(
            src_ref=src, dst_ref=dst, send_sem=send, recv_sem=recv,
            device_id=device, device_id_type=MESH,
        )

    def w_piece(origin, q):
        return wtail.at[origin] if q == 2 else wfull.at[origin, w_rows[q]]

    def w_copy(hop, q, rightward):
        origin = z - hop if rightward else z + hop
        side = 0 if rightward else 1
        target = z + 1 if rightward else z - 1
        ref = w_piece(origin, q)
        return remote(
            ref, ref, w_send.at[side, hop, q], w_recv.at[side, hop, q], (target, e)
        )

    def w_recv_wait(hop, q, rightward):
        origin = z - 1 - hop if rightward else z + 1 + hop
        side = 0 if rightward else 1
        ref = w_piece(origin, q)
        remote(
            ref, ref, w_send.at[side, hop, q], w_recv.at[side, hop, q], (z, peer(SIB))
        ).wait_recv()

    def w_step(hop, h):
        for rightward in (True, False):
            if hop > 0:
                come = z >= hop if rightward else z + hop <= last

                @pl.when(come)
                def _(rightward=rightward):
                    for q in pieces[h]:
                        w_recv_wait(hop - 1, q, rightward)

            if hop < last:
                go = (z >= hop) & (z < last) if rightward else (z + hop <= last) & (z > 0)

                @pl.when(go)
                def _(rightward=rightward):
                    for q in pieces[h]:
                        w_copy(hop, q, rightward).start()

    def g_copy(mask):
        p = peer(mask)
        return remote(gh.at[p], ghr.at[e], g_send.at[mask], g_recv.at[mask], (z, p))

    def chunk_of(step):
        return jnp.where(low, (z + parts - 1 - step) % parts, (z + 1 + step) % parts)

    def c_copy(unit, kind, source, mask, part_of=None):
        c, (first, count) = chunk_of(unit // 2), spans[unit % 2]
        if part_of is not None:
            near = round_up(count // 2, 16)
            first, count = (first, near) if part_of == 0 else (first + near, count - near)
        ref = cg.at[c, peer(source), pl.ds(first, count)]
        return remote(
            ref, ref, c_send.at[unit, kind], c_recv.at[unit, kind], (z, peer(mask))
        )

    def c_copies(unit):
        return [
            c_copy(unit, 0, 0, SIB), c_copy(unit, 1, 0, ALONG_X), c_copy(unit, 2, 0, ALONG_Y),
            c_copy(unit, 3, ALONG_X, ALONG_Y, 0), c_copy(unit, 4, ALONG_Y, ALONG_X, 1),
            c_copy(unit, 5, ALONG_X, SIB), c_copy(unit, 6, ALONG_Y, SIB),
            c_copy(unit, 7, ALONG_X | ALONG_Y, SIB),
        ]

    copies = [c_copies(unit) for unit in range(units)]

    w_step(0, 0)
    w_step(0, 1)

    for load in loads[1:4]:
        load.wait()
    routes = route_ref[...]
    gates = gate_ref[...].astype(jnp.float32)
    scaled = [
        (gates[k : k + 1] * hid_ref[k].astype(jnp.float32)).astype(jnp.bfloat16)
        .astype(jnp.float32)
        for k in range(hid_ref.shape[0])
    ]
    for expert in range(8):
        own = jnp.zeros((ffw, rows), jnp.float32)
        for k, block in enumerate(scaled):
            own = jnp.where(routes[k : k + 1] == expert, block, own)
        own = jnp.concatenate([own, jnp.zeros((tall - ffw, rows), jnp.float32)], axis=0)
        gh[expert] = own.astype(jnp.bfloat16)

    for mask in (6, 2, 4, 1, 3, 5, 7):
        g_copy(mask).start()
    ghr[e] = gh[e]

    for load in loads[4:]:
        load.wait()
    position = lax.broadcasted_iota(jnp.int32, (8, rows), 1)
    scale = jnp.zeros((8, rows), jnp.float32)
    start = 0
    for s in range(len_ref.shape[1]):
        length = len_ref[0, s]
        end = start + length
        ratio = jnp.full((8, rows), adv_ref[0, s]) / jnp.full(
            (8, rows), length.astype(jnp.float32)
        )
        scale = scale + jnp.where((position >= start) & (position < end), ratio, 0.0)
        start = end
    scale = scale[0:1]

    def scale_chunk(step):
        c = chunk_of(step)
        cg[c, e] = (scale * out_ref[c].astype(jnp.float32)).astype(jnp.bfloat16)

    scale_chunk(0)
    for kind in (1, 2, 0):
        copies[0][kind].start()
    for step in range(1, parts):
        scale_chunk(step)

    def gather(unit):
        for kind in (1, 2):
            copies[unit][kind].wait_recv()
        for kind in (3, 4):
            copies[unit][kind].start()
        for later in ((1, 2) if unit == 0 else (unit + 2,)):
            if later < units:
                for kind in (1, 2, 0):
                    copies[later][kind].start()
        for kind in (5, 6):
            copies[unit][kind].start()
        if unit == 0:
            w_step(1, 1)
        for kind in (3, 4):
            copies[unit][kind].wait_recv()
        copies[unit][7].start()
        for kind in (0, 5, 6, 7):
            copies[unit][kind].wait_recv()

    def r_piece(rightward, c, q):
        side = 0 if rightward else 1
        if q == 2:
            src, dst = tailsend.at[c], (tail_left if rightward else tail_right).at[c]
        else:
            src = sendbuf.at[c, :, lanes[q]]
            dst = (from_left if rightward else from_right).at[c, :, lanes[q]]
        return src, dst, r_send.at[side, c, q], r_recv.at[side, c, q]

    def r_copy(c, q, rightward):
        return remote(*r_piece(rightward, c, q), (z + 1 if rightward else z - 1, e))

    def r_wait(c, q, rightward):
        remote(*r_piece(rightward, c, q), (z, peer(SIB))).wait_recv()

    def r_pass(c, h, rightward):
        for q in pieces[h]:
            r_wait(c, q, rightward)
            if q == 2:
                came = (tail_left if rightward else tail_right)[c].astype(jnp.float32)
                tailsend[c] = (tailpart[c] + came).astype(jnp.bfloat16)
            else:
                came = (from_left if rightward else from_right)[c, :, lanes[q]]
                sendbuf[c, :, lanes[q]] = (
                    part[c, :, lanes[q]] + came.astype(jnp.float32)
                ).astype(jnp.bfloat16)
            r_copy(c, q, rightward).start()

    def r_first(c, h, rightward):
        for q in pieces[h]:
            if q == 2:
                tailsend[c] = tailpart[c].astype(jnp.bfloat16)
            else:
                sendbuf[c, :, lanes[q]] = part[c, :, lanes[q]].astype(jnp.bfloat16)
            r_copy(c, q, rightward).start()

    middle = (z > 0) & (z < last)

    def r_farthest(h, near):
        @pl.when(middle & (low if near else jnp.logical_not(low)))
        def _():
            r_pass(last, h, True)

        @pl.when(middle & (jnp.logical_not(low) if near else low))
        def _():
            r_pass(0, h, False)

    w_step(1, 0)
    for unit in range(units):
        gather(unit)
        h = unit % 2
        if unit == 0:
            for mask in range(1, 8):
                g_copy(mask).wait_recv()
            ght[...] = jnp.concatenate([ghr[p] for p in range(8)], axis=1)
        c = chunk_of(unit // 2)
        first, count = spans[h]
        block = jnp.concatenate([cg[c, p, first : first + count] for p in range(8)], axis=1)
        part[c, :, first : first + count] = lax.dot_general(
            ght[...], block, (((1,), (1,)), ((), ())), preferred_element_type=jnp.float32
        )
        if h == 1:
            tailpart[c] = lax.dot_general(
                block[main - first :], ght[...], (((1,), (1,)), ((), ())),
                preferred_element_type=jnp.float32,
            )

        @pl.when((z == 0) & (c > 0))
        def _():
            r_first(c, h, True)

        @pl.when((z == last) & (c < last))
        def _():
            r_first(c, h, False)

        if last > 2:
            if unit == 3:
                w_step(2, 0)
                r_farthest(0, True)
            if unit == 4:
                w_step(2, 1)
            if unit == 5:
                r_farthest(1, True)

    def r_rest(h):
        for i in range(1, last):
            right, left = last - i, i

            @pl.when(middle & (z < right))
            def _(right=right):
                r_pass(right, h, True)

            @pl.when(middle & (z > left))
            def _(left=left):
                r_pass(left, h, False)

    if last > 2:
        r_farthest(0, False)
        r_rest(0)

    far = jnp.where(low, last, 0)

    def back_term(tile, d):
        pair = jnp.concatenate([cg[d, 2 * tile], cg[d, 2 * tile + 1]], axis=1)
        return jnp.dot(
            wfull[d], pair[:main], preferred_element_type=jnp.float32
        ) + jnp.dot(turned[d], pair[main:], preferred_element_type=jnp.float32)

    def b_copy(mask):
        p = peer(mask)
        return remote(backs.at[p], backr.at[e], b_send.at[mask], b_recv.at[mask], (z, p))

    for i in range(1, parts):
        d = (far + i) % parts
        turned[d] = turn(wtail[d]).astype(jnp.bfloat16)

    @pl.loop(0, 4)
    def _(tile):
        total = back_term(tile, (far + 1) % parts)
        for i in range(2, parts):
            total = total + back_term(tile, (far + i) % parts)
        early[tile] = total

    if last > 1:
        w_step(last, 0)
        w_step(last, 1)
    turned[far] = turn(wtail[far]).astype(jnp.bfloat16)
    for mask in (ALONG_X | ALONG_Y, ALONG_X, ALONG_Y, 0):
        tile = peer(mask) // 2
        total = early[tile] + back_term(tile, far)
        total = total.astype(jnp.bfloat16)
        backs[2 * tile] = total[:, :rows]
        backs[2 * tile + 1] = total[:, rows:]
        if mask:
            b_copy(mask).start()
        b_copy(mask | SIB).start()
    backr[e] = backs[e]

    if last > 2:
        r_farthest(1, False)
        r_rest(1)

    for mask in range(1, 8):
        b_copy(mask).wait_recv()
    for k in range(mine_ref.shape[0]):
        mine = jnp.zeros((tall, rows), jnp.float32)
        for expert in range(8):
            mine = jnp.where(routes[k : k + 1] == expert, backr[expert].astype(jnp.float32), mine)
        mine_ref[k] = mine.astype(jnp.bfloat16)

    def r_end(rightward):
        for q in (0, 1, 2):
            r_wait(z, q, rightward)
            if q == 2:
                came = turn((tail_left if rightward else tail_right)[z])
                part[z, :, main:cols] += came
            else:
                came = (from_left if rightward else from_right)[z, :, lanes[q]]
                part[z, :, lanes[q]] += came.astype(jnp.float32)

    @pl.when(z > 0)
    def _():
        r_end(True)

    @pl.when(z < last)
    def _():
        r_end(False)

    gd_ref[...] = part[z, 0:ffw, :]

    for mask in range(1, 8):
        b_copy(mask).wait_send()
        g_copy(mask).wait_send()
    for unit in range(units):
        for copy in copies[unit]:
            copy.wait_send()
    for q in range(3):
        for hop in range(last):

            @pl.when((z >= hop) & (z < last))
            def _():
                w_copy(hop, q, True).wait_send()

            @pl.when((z + hop <= last) & (z > 0))
            def _():
                w_copy(hop, q, False).wait_send()

        for c in range(parts):

            @pl.when(z < c)
            def _():
                r_copy(c, q, True).wait_send()

            @pl.when(z > c)
            def _():
                r_copy(c, q, False).wait_send()


def fused(grad_out, hidden_act, gate_weights, routing, resp_lengths, advantage, w_down):
    rows, width = grad_out.shape
    ffw = hidden_act.shape[2]
    parts = lax.axis_size("dp")
    cols = width // parts
    tall = round_up(ffw, 16)
    topk = routing.shape[1]
    main = cols // 128 * 128
    tail = cols - main
    responses = resp_lengths.shape
    vmem = pl.BlockSpec(memory_space=pltpu.VMEM)
    hbm = pl.BlockSpec(memory_space=pl.ANY)
    dma = pltpu.SemaphoreType.DMA
    bf16, f32 = jnp.bfloat16, jnp.float32
    total, mine = pl.pallas_call(
        functools.partial(exchange_kernel, parts),
        out_shape=(
            jax.ShapeDtypeStruct((ffw, cols), f32),
            jax.ShapeDtypeStruct((topk, tall, rows), bf16),
        ),
        in_specs=[hbm] * 7,
        out_specs=(vmem, vmem),
        scratch_shapes=[
            pltpu.SMEM(responses, jnp.int32),
            pltpu.SMEM(responses, f32),
            pltpu.VMEM((parts, cols, rows), bf16),
            pltpu.VMEM((topk, ffw, rows), bf16),
            pltpu.VMEM((topk, rows), bf16),
            pltpu.VMEM((topk, rows), jnp.int32),
            pltpu.VMEM((ffw, cols), bf16),
            pltpu.VMEM((parts, 8, cols, rows), bf16),
            pltpu.VMEM((4, tall, 2 * rows), f32),
            pltpu.VMEM((8, tall, rows), bf16),
            pltpu.VMEM((8, tall, rows), bf16),
            pltpu.VMEM((8, tall, rows), bf16),
            pltpu.VMEM((tall, 8 * rows), bf16),
            pltpu.VMEM((parts, tall, main), bf16),
            pltpu.VMEM((parts, tall, cols), f32),
            pltpu.VMEM((parts, tall, main), bf16),
            pltpu.VMEM((parts, tall, main), bf16),
            pltpu.VMEM((parts, tall, main), bf16),
            pltpu.VMEM((8, tall, rows), bf16),
            pltpu.VMEM((parts, tail, tall), bf16),
            pltpu.VMEM((parts, tail, tall), f32),
            pltpu.VMEM((parts, tail, tall), bf16),
            pltpu.VMEM((parts, tail, tall), bf16),
            pltpu.VMEM((parts, tail, tall), bf16),
            pltpu.VMEM((parts, tall, tail), bf16),
            dma((2 * parts, 8)), dma((2 * parts, 8)),
            dma((8,)), dma((8,)),
            dma((2, parts, 3)), dma((2, parts, 3)),
            dma((2, parts, 3)), dma((2, parts, 3)),
            dma((8,)), dma((8,)),
            dma((7,)),
        ],
        compiler_params=pltpu.CompilerParams(
            collective_id=0, has_side_effects=True, vmem_limit_bytes=56 * 1024 * 1024
        ),
        cost_estimate=pl.CostEstimate(
            flops=32 * rows * width * tall, bytes_accessed=8 * rows * width * 2, transcendentals=0
        ),
    )(
        resp_lengths, advantage, grad_out.T.reshape(parts, cols, rows),
        hidden_act.transpose(1, 2, 0), gate_weights.T, routing.T, w_down[0],
    )
    mine = mine[:, :ffw].astype(f32).transpose(2, 0, 1)
    grad_down = total[None]
    grad_gates = jnp.sum(mine * hidden_act.astype(f32), axis=2)
    grad_hidden = gate_weights.astype(f32)[:, :, None] * mine
    return (grad_down, grad_hidden, grad_gates)


def solution(mesh):
    fits = mesh.shape["expert"] == 8 and mesh.shape["dp"] == 4
    body = fused if fits else local

    placed = (
        P(("dp", "expert"), None),
        P(("dp", "expert"), None, None),
        P(("dp", "expert"), None),
        P(("dp", "expert"), None),
        P(("dp", "expert"), None),
        P(("dp", "expert"), None),
        P("expert", None, "dp"),
    )
    return jax.shard_map(
        body,
        mesh=mesh,
        in_specs=placed,
        out_specs=(
            P("expert", None, "dp"),
            P(("dp", "expert"), None, None),
            P(("dp", "expert"), None),
        ),
        check_vma=False,
    )
```

```python
import functools

import jax
import jax.numpy as jnp
from jax import lax
from jax.experimental import pallas as pl
from jax.experimental.pallas import tpu as pltpu
from jax.sharding import PartitionSpec as P


def weight_terms(hid_recv, gated):
    partial_term = lax.dot_general(
        hid_recv, gated, (((0,), (0,)), ((), ())), preferred_element_type=jnp.float32
    )
    return lax.psum_scatter(partial_term, "dp", scatter_dimension=1, tiled=True)[None]


def local(grad_out, hidden_act, gate_weights, routing, resp_lengths, advantage, w_down):
    rows = grad_out.shape[0]
    width = grad_out.shape[1]
    topk = routing.shape[1]
    ffw = hidden_act.shape[2]
    nexp = lax.axis_size("expert")
    cap = min(rows, 5 * rows * topk // (4 * nexp))
    items = rows * topk
    slots = nexp * cap
    ends = jnp.cumsum(resp_lengths[0])
    starts = ends - resp_lengths[0]
    position = jnp.arange(rows, dtype=jnp.int32)
    inside = (position[:, None] >= starts[None, :]) & (position[:, None] < ends[None, :])
    ratio = advantage[0] / resp_lengths[0].astype(jnp.float32)
    scale = jnp.sum(jnp.where(inside, ratio[None, :], 0.0), axis=1)
    cotan = (scale[:, None] * grad_out.astype(jnp.float32)).astype(jnp.bfloat16)
    dest = routing.reshape(-1)
    onehot = (dest[:, None] == jnp.arange(nexp, dtype=jnp.int32)[None, :]).astype(jnp.int32)
    rank = jnp.cumsum(onehot, axis=0) - onehot
    place = jnp.sum(rank * onehot, axis=1)
    flat = dest * cap + place
    slot_item = (
        jnp.full((slots,), items, jnp.int32).at[flat].set(jnp.arange(items, dtype=jnp.int32))
    )
    valid = slot_item < items
    safe = jnp.minimum(slot_item, items - 1)
    send_cot = jnp.where(valid[:, None], cotan[safe // topk], jnp.zeros((), jnp.bfloat16))
    send_hid = jnp.where(
        valid[:, None], hidden_act.reshape(items, ffw)[safe], jnp.zeros((), jnp.bfloat16)
    )
    send_gate = jnp.where(valid, gate_weights.reshape(items)[safe], jnp.zeros((), jnp.bfloat16))
    recv_cot, recv_hid, recv_gate = (
        lax.all_to_all(
            send_cot.reshape(nexp, cap, width), "expert", split_axis=0, concat_axis=0, tiled=True
        ),
        lax.all_to_all(
            send_hid.reshape(nexp, cap, ffw), "expert", split_axis=0, concat_axis=0, tiled=True
        ),
        lax.all_to_all(
            send_gate.reshape(nexp, cap), "expert", split_axis=0, concat_axis=0, tiled=True
        ),
    )
    recv_cot = recv_cot.reshape(slots, width)
    recv_hid = recv_hid.reshape(slots, ffw)
    recv_gate = recv_gate.reshape(slots).astype(jnp.float32)
    gated = (recv_gate[:, None] * recv_cot.astype(jnp.float32)).astype(jnp.bfloat16)
    local_weight = w_down[0]
    piece = lax.all_gather(local_weight, "dp", axis=1, tiled=True)
    back_sum = lax.dot_general(
        recv_cot, piece, (((1,), (1,)), ((), ())), preferred_element_type=jnp.float32
    )
    output = jnp.dot(recv_hid, piece, preferred_element_type=jnp.float32)
    gate_sum = jnp.sum(recv_cot.astype(jnp.float32) * output, axis=1)
    dhid = recv_gate[:, None] * back_sum
    result_hid, result_gate = (
        lax.all_to_all(
            dhid.reshape(nexp, cap, ffw), "expert", split_axis=0, concat_axis=0, tiled=True
        ),
        lax.all_to_all(
            gate_sum.reshape(nexp, cap), "expert", split_axis=0, concat_axis=0, tiled=True
        ),
    )
    grad_down = weight_terms(recv_hid, gated)
    grad_hidden = result_hid.reshape(slots, ffw)[flat].reshape(rows, topk, ffw)
    grad_gates = result_gate.reshape(slots)[flat].reshape(rows, topk)
    return (grad_down, grad_hidden, grad_gates)


MESH = pl.DeviceIdType.MESH
SIB, ALONG_X, ALONG_Y = 1, 2, 4


def round_up(size, unit):
    return -(-size // unit) * unit


def exchange_kernel(
    parts, len_hbm, adv_hbm, out_hbm, hid_hbm, gate_hbm, route_hbm, w_hbm, gd_ref, mine_ref,
    len_ref, adv_ref, out_ref, hid_ref, gate_ref, route_ref, w_ref,
    cg, early, gh, backr, ghr, ght, wfull, part, sendbuf, from_left, from_right, backs,
    c_send, c_recv, g_send, g_recv, w_send, w_recv, r_send, r_recv, b_send, b_recv, in_sem,
):
    z = lax.axis_index("dp")
    e = lax.axis_index("expert")
    core, xpos, ypos = e % 2, (e // 2) % 2, e // 4
    last = parts - 1
    cols, rows = out_ref.shape[1:]
    ffw = hid_ref.shape[1]
    tall = gh.shape[1]
    split = min(cols, round_up(cols // 2, 128))
    spans = ((0, split), (split, cols - split))
    lanes = (pl.ds(0, split), pl.ds(split, part.shape[2] - split))
    w_half = round_up(tall // 2, 16)
    w_rows = (pl.ds(0, w_half), pl.ds(w_half, tall - w_half))
    units = 2 * parts
    loads = [
        pltpu.make_async_copy(src, dst, in_sem.at[i])
        for i, (src, dst) in enumerate((
            (w_hbm, w_ref), (route_hbm, route_ref), (gate_hbm, gate_ref), (hid_hbm, hid_ref),
            (len_hbm, len_ref), (adv_hbm, adv_ref), (out_hbm, out_ref),
        ))
    ]
    for load in loads:
        load.start()
    low = 2 * z < parts

    def peer(mask):
        c = 1 - core if mask & 1 else core
        x = 1 - xpos if mask & 2 else xpos
        y = 1 - ypos if mask & 4 else ypos
        return (y * 2 + x) * 2 + c

    barrier = pltpu.get_barrier_semaphore()
    for mask in range(1, 8):
        pl.semaphore_signal(barrier, inc=1, device_id=(z, peer(mask)), device_id_type=MESH)

    @pl.when(z > 0)
    def _():
        pl.semaphore_signal(barrier, inc=1, device_id=(z - 1, e), device_id_type=MESH)

    @pl.when(z < last)
    def _():
        pl.semaphore_signal(barrier, inc=1, device_id=(z + 1, e), device_id_type=MESH)

    wfull[z] = jnp.zeros(wfull.shape[1:], jnp.bfloat16)
    loads[0].wait()
    wfull[z, 0:ffw, 0:cols] = w_ref[...]
    pl.semaphore_wait(barrier, 7 + jnp.minimum(z, 1) + jnp.minimum(last - z, 1))

    def remote(src, dst, send, recv, device):
        return pltpu.make_async_remote_copy(
            src_ref=src, dst_ref=dst, send_sem=send, recv_sem=recv,
            device_id=device, device_id_type=MESH,
        )

    def w_copy(hop, h, rightward):
        origin = z - hop if rightward else z + hop
        side = 0 if rightward else 1
        target = z + 1 if rightward else z - 1
        ref = wfull.at[origin, w_rows[h]]
        return remote(
            ref, ref, w_send.at[side, hop, h], w_recv.at[side, hop, h], (target, e)
        )

    def w_recv_wait(hop, h, rightward):
        origin = z - 1 - hop if rightward else z + 1 + hop
        side = 0 if rightward else 1
        ref = wfull.at[origin, w_rows[h]]
        remote(
            ref, ref, w_send.at[side, hop, h], w_recv.at[side, hop, h], (z, peer(SIB))
        ).wait_recv()

    def w_step(hop, h):
        for rightward in (True, False):
            if hop > 0:
                come = z >= hop if rightward else z + hop <= last

                @pl.when(come)
                def _(rightward=rightward):
                    w_recv_wait(hop - 1, h, rightward)

            if hop < last:
                go = (z >= hop) & (z < last) if rightward else (z + hop <= last) & (z > 0)

                @pl.when(go)
                def _(rightward=rightward):
                    w_copy(hop, h, rightward).start()

    def g_copy(mask):
        p = peer(mask)
        return remote(gh.at[p], ghr.at[e], g_send.at[mask], g_recv.at[mask], (z, p))

    def chunk_of(step):
        return jnp.where(low, (z + parts - 1 - step) % parts, (z + 1 + step) % parts)

    def c_copy(unit, kind, source, mask, part_of=None):
        c, (first, count) = chunk_of(unit // 2), spans[unit % 2]
        if part_of is not None:
            near = round_up(count // 2, 16)
            first, count = (first, near) if part_of == 0 else (first + near, count - near)
        ref = cg.at[c, peer(source), pl.ds(first, count)]
        return remote(
            ref, ref, c_send.at[unit, kind], c_recv.at[unit, kind], (z, peer(mask))
        )

    def c_copies(unit):
        return [
            c_copy(unit, 0, 0, SIB), c_copy(unit, 1, 0, ALONG_X), c_copy(unit, 2, 0, ALONG_Y),
            c_copy(unit, 3, ALONG_X, ALONG_Y, 0), c_copy(unit, 4, ALONG_Y, ALONG_X, 1),
            c_copy(unit, 5, ALONG_X, SIB), c_copy(unit, 6, ALONG_Y, SIB),
            c_copy(unit, 7, ALONG_X | ALONG_Y, SIB),
        ]

    copies = [c_copies(unit) for unit in range(units)]

    w_step(0, 0)
    w_step(0, 1)

    for load in loads[1:4]:
        load.wait()
    routes = route_ref[...]
    gates = gate_ref[...].astype(jnp.float32)
    scaled = [
        (gates[k : k + 1] * hid_ref[k].astype(jnp.float32)).astype(jnp.bfloat16)
        .astype(jnp.float32)
        for k in range(hid_ref.shape[0])
    ]
    for expert in range(8):
        own = jnp.zeros((ffw, rows), jnp.float32)
        for k, block in enumerate(scaled):
            own = jnp.where(routes[k : k + 1] == expert, block, own)
        own = jnp.concatenate([own, jnp.zeros((tall - ffw, rows), jnp.float32)], axis=0)
        gh[expert] = own.astype(jnp.bfloat16)

    for mask in (6, 2, 4, 1, 3, 5, 7):
        g_copy(mask).start()
    ghr[e] = gh[e]

    for load in loads[4:]:
        load.wait()
    position = lax.broadcasted_iota(jnp.int32, (8, rows), 1)
    scale = jnp.zeros((8, rows), jnp.float32)
    start = 0
    for s in range(len_ref.shape[1]):
        length = len_ref[0, s]
        end = start + length
        ratio = jnp.full((8, rows), adv_ref[0, s]) / jnp.full(
            (8, rows), length.astype(jnp.float32)
        )
        scale = scale + jnp.where((position >= start) & (position < end), ratio, 0.0)
        start = end
    scale = scale[0:1]

    def scale_chunk(step):
        c = chunk_of(step)
        cg[c, e] = (scale * out_ref[c].astype(jnp.float32)).astype(jnp.bfloat16)

    scale_chunk(0)
    for kind in (1, 2, 0):
        copies[0][kind].start()
    for kind in (1, 2, 0):
        copies[1][kind].start()
    for step in range(1, parts):
        scale_chunk(step)

    def gather_near(unit):
        for kind in (1, 2):
            copies[unit][kind].wait_recv()
        for kind in (3, 4, 5, 6):
            copies[unit][kind].start()
        if unit + 2 < units:
            for kind in (1, 2, 0):
                copies[unit + 2][kind].start()

    def gather_far(unit):
        for kind in (3, 4):
            copies[unit][kind].wait_recv()
        copies[unit][7].start()

    def gather_end(unit):
        for kind in (0, 5, 6, 7):
            copies[unit][kind].wait_recv()

    def r_copy(c, h, rightward):
        side = 0 if rightward else 1
        dst = from_left if rightward else from_right
        return remote(
            sendbuf.at[c, :, lanes[h]], dst.at[c, :, lanes[h]],
            r_send.at[side, c, h], r_recv.at[side, c, h],
            (z + 1 if rightward else z - 1, e),
        )

    def r_wait(c, h, rightward):
        side = 0 if rightward else 1
        dst = from_left if rightward else from_right
        remote(
            sendbuf.at[c, :, lanes[h]], dst.at[c, :, lanes[h]],
            r_send.at[side, c, h], r_recv.at[side, c, h], (z, peer(SIB)),
        ).wait_recv()

    def r_pass(c, h, rightward):
        r_wait(c, h, rightward)
        came = (from_left if rightward else from_right)[c, :, lanes[h]].astype(jnp.float32)
        sendbuf[c, :, lanes[h]] = (part[c, :, lanes[h]] + came).astype(sendbuf.dtype)
        r_copy(c, h, rightward).start()

    def r_first(c, h, rightward):
        sendbuf[c, :, lanes[h]] = part[c, :, lanes[h]].astype(sendbuf.dtype)
        r_copy(c, h, rightward).start()

    middle = (z > 0) & (z < last)

    def r_farthest(h, near):
        @pl.when(middle & (low if near else jnp.logical_not(low)))
        def _():
            r_pass(last, h, True)

        @pl.when(middle & (jnp.logical_not(low) if near else low))
        def _():
            r_pass(0, h, False)

    w_step(1, 0)
    gather_near(0)
    gather_near(1)
    w_step(1, 1)
    gather_far(0)
    for unit in range(units):
        if unit >= 1 and unit + 2 < units:
            gather_near(unit + 2)
        if unit >= 1 and unit + 1 < units:
            gather_far(unit + 1)
        gather_end(unit)
        h = unit % 2
        if unit == 0:
            for mask in range(1, 8):
                g_copy(mask).wait_recv()
            ght[...] = jnp.concatenate([ghr[p] for p in range(8)], axis=1)
        c = chunk_of(unit // 2)
        first, count = spans[h]
        block = jnp.concatenate([cg[c, p, first : first + count] for p in range(8)], axis=1)
        part[c, :, first : first + count] = lax.dot_general(
            ght[...], block, (((1,), (1,)), ((), ())), preferred_element_type=jnp.float32
        )

        @pl.when((z == 0) & (c > 0))
        def _():
            r_first(c, h, True)

        @pl.when((z == last) & (c < last))
        def _():
            r_first(c, h, False)

        if unit == 0:
            gather_near(2)
            gather_far(1)
        if last > 2:
            if unit == 3:
                w_step(2, 0)
                r_farthest(0, True)
            if unit == 4:
                w_step(2, 1)
            if unit == 5:
                r_farthest(1, True)

    def r_rest(h):
        for i in range(1, last):
            right, left = last - i, i

            @pl.when(middle & (z < right))
            def _(right=right):
                r_pass(right, h, True)

            @pl.when(middle & (z > left))
            def _(left=left):
                r_pass(left, h, False)

    if last > 2:
        r_farthest(0, False)
        r_rest(0)

    far = jnp.where(low, last, 0)

    def back_term(tile, d):
        pair = jnp.concatenate([cg[d, 2 * tile], cg[d, 2 * tile + 1]], axis=1)
        return jnp.dot(wfull[d][:, :cols], pair, preferred_element_type=jnp.float32)

    def b_copy(mask):
        p = peer(mask)
        return remote(backs.at[p], backr.at[e], b_send.at[mask], b_recv.at[mask], (z, p))

    @pl.loop(0, 4)
    def _(tile):
        total = back_term(tile, (far + 1) % parts)
        for i in range(2, parts):
            total = total + back_term(tile, (far + i) % parts)
        early[tile] = total

    if last > 1:
        w_step(last, 0)
        w_step(last, 1)
    for mask in (ALONG_X | ALONG_Y, ALONG_X, ALONG_Y, 0):
        tile = peer(mask) // 2
        total = early[tile] + back_term(tile, far)
        total = total.astype(jnp.bfloat16)
        backs[2 * tile] = total[:, :rows]
        backs[2 * tile + 1] = total[:, rows:]
        if mask:
            b_copy(mask).start()
        b_copy(mask | SIB).start()
    backr[e] = backs[e]

    if last > 2:
        r_farthest(1, False)
        r_rest(1)

    for mask in range(1, 8):
        b_copy(mask).wait_recv()
    for k in range(mine_ref.shape[0]):
        mine = jnp.zeros((tall, rows), jnp.float32)
        for expert in range(8):
            mine = jnp.where(routes[k : k + 1] == expert, backr[expert].astype(jnp.float32), mine)
        mine_ref[k] = mine.astype(jnp.bfloat16)

    for h, (first, count) in enumerate(spans):

        @pl.when(z > 0)
        def _(h=h):
            r_wait(z, h, True)
            part[z, :, lanes[h]] += from_left[z, :, lanes[h]].astype(jnp.float32)

        @pl.when(z < last)
        def _(h=h):
            r_wait(z, h, False)
            part[z, :, lanes[h]] += from_right[z, :, lanes[h]].astype(jnp.float32)

        gd_ref[:, first : first + count] = part[z, 0:ffw, first : first + count]

    for mask in range(1, 8):
        b_copy(mask).wait_send()
        g_copy(mask).wait_send()
    for unit in range(units):
        for copy in copies[unit]:
            copy.wait_send()
    for h in range(2):
        for hop in range(last):

            @pl.when((z >= hop) & (z < last))
            def _():
                w_copy(hop, h, True).wait_send()

            @pl.when((z + hop <= last) & (z > 0))
            def _():
                w_copy(hop, h, False).wait_send()

        for c in range(parts):

            @pl.when(z < c)
            def _():
                r_copy(c, h, True).wait_send()

            @pl.when(z > c)
            def _():
                r_copy(c, h, False).wait_send()


def fused(grad_out, hidden_act, gate_weights, routing, resp_lengths, advantage, w_down):
    rows, width = grad_out.shape
    ffw = hidden_act.shape[2]
    parts = lax.axis_size("dp")
    cols = width // parts
    tall = round_up(ffw, 16)
    topk = routing.shape[1]
    wide = round_up(cols, 128)
    responses = resp_lengths.shape
    vmem = pl.BlockSpec(memory_space=pltpu.VMEM)
    hbm = pl.BlockSpec(memory_space=pl.ANY)
    dma = pltpu.SemaphoreType.DMA
    bf16, f32 = jnp.bfloat16, jnp.float32
    total, mine = pl.pallas_call(
        functools.partial(exchange_kernel, parts),
        out_shape=(
            jax.ShapeDtypeStruct((ffw, cols), f32),
            jax.ShapeDtypeStruct((topk, tall, rows), bf16),
        ),
        in_specs=[hbm] * 7,
        out_specs=(vmem, vmem),
        scratch_shapes=[
            pltpu.SMEM(responses, jnp.int32),
            pltpu.SMEM(responses, f32),
            pltpu.VMEM((parts, cols, rows), bf16),
            pltpu.VMEM((topk, ffw, rows), bf16),
            pltpu.VMEM((topk, rows), bf16),
            pltpu.VMEM((topk, rows), jnp.int32),
            pltpu.VMEM((ffw, cols), bf16),
            pltpu.VMEM((parts, 8, cols, rows), bf16),
            pltpu.VMEM((4, tall, 2 * rows), f32),
            pltpu.VMEM((8, tall, rows), bf16),
            pltpu.VMEM((8, tall, rows), bf16),
            pltpu.VMEM((8, tall, rows), bf16),
            pltpu.VMEM((tall, 8 * rows), bf16),
            pltpu.VMEM((parts, tall, wide), bf16),
            pltpu.VMEM((parts, tall, wide), f32),
            pltpu.VMEM((parts, tall, wide), bf16),
            pltpu.VMEM((parts, tall, wide), bf16),
            pltpu.VMEM((parts, tall, wide), bf16),
            pltpu.VMEM((8, tall, rows), bf16),
            dma((2 * parts, 8)), dma((2 * parts, 8)),
            dma((8,)), dma((8,)),
            dma((2, parts, 2)), dma((2, parts, 2)),
            dma((2, parts, 2)), dma((2, parts, 2)),
            dma((8,)), dma((8,)),
            dma((7,)),
        ],
        compiler_params=pltpu.CompilerParams(
            collective_id=0, has_side_effects=True, vmem_limit_bytes=56 * 1024 * 1024
        ),
        cost_estimate=pl.CostEstimate(
            flops=32 * rows * width * tall, bytes_accessed=8 * rows * width * 2, transcendentals=0
        ),
    )(
        resp_lengths, advantage, grad_out.T.reshape(parts, cols, rows),
        hidden_act.transpose(1, 2, 0), gate_weights.T, routing.T, w_down[0],
    )
    mine = mine[:, :ffw].astype(f32).transpose(2, 0, 1)
    grad_down = total[None]
    grad_gates = jnp.sum(mine * hidden_act.astype(f32), axis=2)
    grad_hidden = gate_weights.astype(f32)[:, :, None] * mine
    return (grad_down, grad_hidden, grad_gates)


def solution(mesh):
    fits = mesh.shape["expert"] == 8 and mesh.shape["dp"] == 4
    body = fused if fits else local

    placed = (
        P(("dp", "expert"), None),
        P(("dp", "expert"), None, None),
        P(("dp", "expert"), None),
        P(("dp", "expert"), None),
        P(("dp", "expert"), None),
        P(("dp", "expert"), None),
        P("expert", None, "dp"),
    )
    return jax.shard_map(
        body,
        mesh=mesh,
        in_specs=placed,
        out_specs=(
            P("expert", None, "dp"),
            P(("dp", "expert"), None, None),
            P(("dp", "expert"), None),
        ),
        check_vma=False,
    )
```

```python
import functools

import jax
import jax.numpy as jnp
from jax import lax
from jax.experimental import pallas as pl
from jax.experimental.pallas import tpu as pltpu
from jax.sharding import PartitionSpec as P


def weight_terms(hid_recv, gated):
    partial_term = lax.dot_general(
        hid_recv, gated, (((0,), (0,)), ((), ())), preferred_element_type=jnp.float32
    )
    return lax.psum_scatter(partial_term, "dp", scatter_dimension=1, tiled=True)[None]


def local(grad_out, hidden_act, gate_weights, routing, resp_lengths, advantage, w_down):
    rows = grad_out.shape[0]
    width = grad_out.shape[1]
    topk = routing.shape[1]
    ffw = hidden_act.shape[2]
    nexp = lax.axis_size("expert")
    cap = min(rows, 5 * rows * topk // (4 * nexp))
    items = rows * topk
    slots = nexp * cap
    ends = jnp.cumsum(resp_lengths[0])
    starts = ends - resp_lengths[0]
    position = jnp.arange(rows, dtype=jnp.int32)
    inside = (position[:, None] >= starts[None, :]) & (position[:, None] < ends[None, :])
    ratio = advantage[0] / resp_lengths[0].astype(jnp.float32)
    scale = jnp.sum(jnp.where(inside, ratio[None, :], 0.0), axis=1)
    cotan = (scale[:, None] * grad_out.astype(jnp.float32)).astype(jnp.bfloat16)
    dest = routing.reshape(-1)
    onehot = (dest[:, None] == jnp.arange(nexp, dtype=jnp.int32)[None, :]).astype(jnp.int32)
    rank = jnp.cumsum(onehot, axis=0) - onehot
    place = jnp.sum(rank * onehot, axis=1)
    flat = dest * cap + place
    slot_item = (
        jnp.full((slots,), items, jnp.int32).at[flat].set(jnp.arange(items, dtype=jnp.int32))
    )
    valid = slot_item < items
    safe = jnp.minimum(slot_item, items - 1)
    send_cot = jnp.where(valid[:, None], cotan[safe // topk], jnp.zeros((), jnp.bfloat16))
    send_hid = jnp.where(
        valid[:, None], hidden_act.reshape(items, ffw)[safe], jnp.zeros((), jnp.bfloat16)
    )
    send_gate = jnp.where(valid, gate_weights.reshape(items)[safe], jnp.zeros((), jnp.bfloat16))
    recv_cot, recv_hid, recv_gate = (
        lax.all_to_all(
            send_cot.reshape(nexp, cap, width), "expert", split_axis=0, concat_axis=0, tiled=True
        ),
        lax.all_to_all(
            send_hid.reshape(nexp, cap, ffw), "expert", split_axis=0, concat_axis=0, tiled=True
        ),
        lax.all_to_all(
            send_gate.reshape(nexp, cap), "expert", split_axis=0, concat_axis=0, tiled=True
        ),
    )
    recv_cot = recv_cot.reshape(slots, width)
    recv_hid = recv_hid.reshape(slots, ffw)
    recv_gate = recv_gate.reshape(slots).astype(jnp.float32)
    gated = (recv_gate[:, None] * recv_cot.astype(jnp.float32)).astype(jnp.bfloat16)
    local_weight = w_down[0]
    piece = lax.all_gather(local_weight, "dp", axis=1, tiled=True)
    back_sum = lax.dot_general(
        recv_cot, piece, (((1,), (1,)), ((), ())), preferred_element_type=jnp.float32
    )
    output = jnp.dot(recv_hid, piece, preferred_element_type=jnp.float32)
    gate_sum = jnp.sum(recv_cot.astype(jnp.float32) * output, axis=1)
    dhid = recv_gate[:, None] * back_sum
    result_hid, result_gate = (
        lax.all_to_all(
            dhid.reshape(nexp, cap, ffw), "expert", split_axis=0, concat_axis=0, tiled=True
        ),
        lax.all_to_all(
            gate_sum.reshape(nexp, cap), "expert", split_axis=0, concat_axis=0, tiled=True
        ),
    )
    grad_down = weight_terms(recv_hid, gated)
    grad_hidden = result_hid.reshape(slots, ffw)[flat].reshape(rows, topk, ffw)
    grad_gates = result_gate.reshape(slots)[flat].reshape(rows, topk)
    return (grad_down, grad_hidden, grad_gates)


MESH = pl.DeviceIdType.MESH
SIB, ALONG_X, ALONG_Y = 1, 2, 4


def round_up(size, unit):
    return -(-size // unit) * unit


def exchange_kernel(
    parts, len_hbm, adv_hbm, out_hbm, hid_hbm, gate_hbm, route_hbm, w_hbm, gd_ref, mine_ref,
    len_ref, adv_ref, out_ref, hid_ref, gate_ref, route_ref, w_ref,
    cg, early, gh, backr, ghr, ght, wfull, part, sendbuf, from_left, from_right, backs,
    wtail, tailpart, tailsend, tail_left, tail_right, turned,
    c_send, c_recv, g_send, g_recv, w_send, w_recv, r_send, r_recv, b_send, b_recv, in_sem,
):
    z = lax.axis_index("dp")
    e = lax.axis_index("expert")
    core, xpos, ypos = e % 2, (e // 2) % 2, e // 4
    last = parts - 1
    cols, rows = out_ref.shape[1:]
    ffw = hid_ref.shape[1]
    tall = gh.shape[1]
    split = min(cols, round_up(cols // 2, 128))
    spans = ((0, split), (split, cols - split))
    main = wfull.shape[2]
    tail = cols - main
    lanes = (pl.ds(0, split), pl.ds(split, main - split))
    w_half = round_up((tall * main + tail * tall) // (2 * main), 16)
    w_rows = (pl.ds(0, w_half), pl.ds(w_half, tall - w_half))
    pieces = ((0,), (1, 2))
    units = 2 * parts
    loads = [
        pltpu.make_async_copy(src, dst, in_sem.at[i])
        for i, (src, dst) in enumerate((
            (w_hbm, w_ref), (route_hbm, route_ref), (gate_hbm, gate_ref), (hid_hbm, hid_ref),
            (len_hbm, len_ref), (adv_hbm, adv_ref), (out_hbm, out_ref),
        ))
    ]
    for load in loads:
        load.start()
    low = 2 * z < parts

    def peer(mask):
        c = 1 - core if mask & 1 else core
        x = 1 - xpos if mask & 2 else xpos
        y = 1 - ypos if mask & 4 else ypos
        return (y * 2 + x) * 2 + c

    barrier = pltpu.get_barrier_semaphore()
    for mask in range(1, 8):
        pl.semaphore_signal(barrier, inc=1, device_id=(z, peer(mask)), device_id_type=MESH)

    @pl.when(z > 0)
    def _():
        pl.semaphore_signal(barrier, inc=1, device_id=(z - 1, e), device_id_type=MESH)

    @pl.when(z < last)
    def _():
        pl.semaphore_signal(barrier, inc=1, device_id=(z + 1, e), device_id_type=MESH)

    loads[0].wait()
    own_w = jnp.concatenate([w_ref[...], jnp.zeros((tall - ffw, cols), jnp.bfloat16)], axis=0)
    wfull[z] = own_w[:, :main]
    chosen = (
        lax.broadcasted_iota(jnp.int32, (tail, cols), 0) + main
        == lax.broadcasted_iota(jnp.int32, (tail, cols), 1)
    ).astype(jnp.float32).astype(jnp.bfloat16)
    wtail[z] = lax.dot_general(
        chosen, own_w, (((1,), (1,)), ((), ())), preferred_element_type=jnp.float32
    ).astype(jnp.bfloat16)
    eye = (
        lax.broadcasted_iota(jnp.int32, (tall, tall), 0)
        == lax.broadcasted_iota(jnp.int32, (tall, tall), 1)
    ).astype(jnp.float32).astype(jnp.bfloat16)

    def turn(block):
        return lax.dot_general(
            eye, block, (((1,), (1,)), ((), ())), preferred_element_type=jnp.float32
        )

    pl.semaphore_wait(barrier, 7 + jnp.minimum(z, 1) + jnp.minimum(last - z, 1))

    def remote(src, dst, send, recv, device):
        return pltpu.make_async_remote_copy(
            src_ref=src, dst_ref=dst, send_sem=send, recv_sem=recv,
            device_id=device, device_id_type=MESH,
        )

    def w_piece(origin, q):
        return wtail.at[origin] if q == 2 else wfull.at[origin, w_rows[q]]

    def w_copy(hop, q, rightward):
        origin = z - hop if rightward else z + hop
        side = 0 if rightward else 1
        target = z + 1 if rightward else z - 1
        ref = w_piece(origin, q)
        return remote(
            ref, ref, w_send.at[side, hop, q], w_recv.at[side, hop, q], (target, e)
        )

    def w_recv_wait(hop, q, rightward):
        origin = z - 1 - hop if rightward else z + 1 + hop
        side = 0 if rightward else 1
        ref = w_piece(origin, q)
        remote(
            ref, ref, w_send.at[side, hop, q], w_recv.at[side, hop, q], (z, peer(SIB))
        ).wait_recv()

    def w_step(hop, h):
        for rightward in (True, False):
            if hop > 0:
                come = z >= hop if rightward else z + hop <= last

                @pl.when(come)
                def _(rightward=rightward):
                    for q in pieces[h]:
                        w_recv_wait(hop - 1, q, rightward)

            if hop < last:
                go = (z >= hop) & (z < last) if rightward else (z + hop <= last) & (z > 0)

                @pl.when(go)
                def _(rightward=rightward):
                    for q in pieces[h]:
                        w_copy(hop, q, rightward).start()

    def g_copy(mask):
        p = peer(mask)
        return remote(gh.at[p], ghr.at[e], g_send.at[mask], g_recv.at[mask], (z, p))

    def chunk_of(step):
        return jnp.where(low, (z + parts - 1 - step) % parts, (z + 1 + step) % parts)

    def c_copy(unit, kind, source, mask, part_of=None):
        c, (first, count) = chunk_of(unit // 2), spans[unit % 2]
        if part_of is not None:
            near = round_up(count // 2, 16)
            first, count = (first, near) if part_of == 0 else (first + near, count - near)
        ref = cg.at[c, peer(source), pl.ds(first, count)]
        return remote(
            ref, ref, c_send.at[unit, kind], c_recv.at[unit, kind], (z, peer(mask))
        )

    def c_copies(unit):
        return [
            c_copy(unit, 0, 0, SIB), c_copy(unit, 1, 0, ALONG_X), c_copy(unit, 2, 0, ALONG_Y),
            c_copy(unit, 3, ALONG_X, ALONG_Y, 0), c_copy(unit, 4, ALONG_Y, ALONG_X, 1),
            c_copy(unit, 5, ALONG_X, SIB), c_copy(unit, 6, ALONG_Y, SIB),
            c_copy(unit, 7, ALONG_X | ALONG_Y, SIB),
        ]

    copies = [c_copies(unit) for unit in range(units)]

    w_step(0, 0)
    w_step(0, 1)

    for load in loads[1:4]:
        load.wait()
    routes = route_ref[...]
    gates = gate_ref[...].astype(jnp.float32)
    scaled = [
        (gates[k : k + 1] * hid_ref[k].astype(jnp.float32)).astype(jnp.bfloat16)
        .astype(jnp.float32)
        for k in range(hid_ref.shape[0])
    ]
    for expert in range(8):
        own = jnp.zeros((ffw, rows), jnp.float32)
        for k, block in enumerate(scaled):
            own = jnp.where(routes[k : k + 1] == expert, block, own)
        own = jnp.concatenate([own, jnp.zeros((tall - ffw, rows), jnp.float32)], axis=0)
        gh[expert] = own.astype(jnp.bfloat16)

    for mask in (6, 2, 4, 1, 3, 5, 7):
        g_copy(mask).start()
    ghr[e] = gh[e]

    for load in loads[4:]:
        load.wait()
    position = lax.broadcasted_iota(jnp.int32, (8, rows), 1)
    scale = jnp.zeros((8, rows), jnp.float32)
    start = 0
    for s in range(len_ref.shape[1]):
        length = len_ref[0, s]
        end = start + length
        ratio = jnp.full((8, rows), adv_ref[0, s]) / jnp.full(
            (8, rows), length.astype(jnp.float32)
        )
        scale = scale + jnp.where((position >= start) & (position < end), ratio, 0.0)
        start = end
    scale = scale[0:1]

    def scale_chunk(step):
        c = chunk_of(step)
        cg[c, e] = (scale * out_ref[c].astype(jnp.float32)).astype(jnp.bfloat16)

    scale_chunk(0)
    for kind in (1, 2, 0):
        copies[0][kind].start()
    for kind in (1, 2, 0):
        copies[1][kind].start()
    for step in range(1, parts):
        scale_chunk(step)

    def gather_near(unit):
        for kind in (1, 2):
            copies[unit][kind].wait_recv()
        for kind in (3, 4, 5, 6):
            copies[unit][kind].start()
        if unit + 2 < units:
            for kind in (1, 2, 0):
                copies[unit + 2][kind].start()

    def gather_far(unit):
        for kind in (3, 4):
            copies[unit][kind].wait_recv()
        copies[unit][7].start()

    def gather_end(unit):
        for kind in (0, 5, 6, 7):
            copies[unit][kind].wait_recv()

    def r_piece(rightward, c, q):
        side = 0 if rightward else 1
        if q == 2:
            src, dst = tailsend.at[c], (tail_left if rightward else tail_right).at[c]
        else:
            src = sendbuf.at[c, :, lanes[q]]
            dst = (from_left if rightward else from_right).at[c, :, lanes[q]]
        return src, dst, r_send.at[side, c, q], r_recv.at[side, c, q]

    def r_copy(c, q, rightward):
        return remote(*r_piece(rightward, c, q), (z + 1 if rightward else z - 1, e))

    def r_wait(c, q, rightward):
        remote(*r_piece(rightward, c, q), (z, peer(SIB))).wait_recv()

    def r_pass(c, h, rightward):
        for q in pieces[h]:
            r_wait(c, q, rightward)
            if q == 2:
                came = (tail_left if rightward else tail_right)[c].astype(jnp.float32)
                tailsend[c] = (tailpart[c] + came).astype(jnp.bfloat16)
            else:
                came = (from_left if rightward else from_right)[c, :, lanes[q]]
                sendbuf[c, :, lanes[q]] = (
                    part[c, :, lanes[q]] + came.astype(jnp.float32)
                ).astype(jnp.bfloat16)
            r_copy(c, q, rightward).start()

    def r_first(c, h, rightward):
        for q in pieces[h]:
            if q == 2:
                tailsend[c] = tailpart[c].astype(jnp.bfloat16)
            else:
                sendbuf[c, :, lanes[q]] = part[c, :, lanes[q]].astype(jnp.bfloat16)
            r_copy(c, q, rightward).start()

    middle = (z > 0) & (z < last)

    def r_farthest(h, near):
        @pl.when(middle & (low if near else jnp.logical_not(low)))
        def _():
            r_pass(last, h, True)

        @pl.when(middle & (jnp.logical_not(low) if near else low))
        def _():
            r_pass(0, h, False)

    w_step(1, 0)
    gather_near(0)
    gather_near(1)
    w_step(1, 1)
    gather_far(0)
    for unit in range(units):
        if unit >= 1 and unit + 2 < units:
            gather_near(unit + 2)
        if unit >= 1 and unit + 1 < units:
            gather_far(unit + 1)
        gather_end(unit)
        h = unit % 2
        if unit == 0:
            for mask in range(1, 8):
                g_copy(mask).wait_recv()
            ght[...] = jnp.concatenate([ghr[p] for p in range(8)], axis=1)
        c = chunk_of(unit // 2)
        first, count = spans[h]
        block = jnp.concatenate([cg[c, p, first : first + count] for p in range(8)], axis=1)
        part[c, :, first : first + count] = lax.dot_general(
            ght[...], block, (((1,), (1,)), ((), ())), preferred_element_type=jnp.float32
        )
        if h == 1:
            tailpart[c] = lax.dot_general(
                block[main - first :], ght[...], (((1,), (1,)), ((), ())),
                preferred_element_type=jnp.float32,
            )

        @pl.when((z == 0) & (c > 0))
        def _():
            r_first(c, h, True)

        @pl.when((z == last) & (c < last))
        def _():
            r_first(c, h, False)

        if unit == 0:
            gather_near(2)
            gather_far(1)
        if last > 2:
            if unit == 3:
                w_step(2, 0)
                r_farthest(0, True)
            if unit == 4:
                w_step(2, 1)
            if unit == 5:
                r_farthest(1, True)

    def r_rest(h):
        for i in range(1, last):
            right, left = last - i, i

            @pl.when(middle & (z < right))
            def _(right=right):
                r_pass(right, h, True)

            @pl.when(middle & (z > left))
            def _(left=left):
                r_pass(left, h, False)

    if last > 2:
        r_farthest(0, False)
        r_rest(0)

    far = jnp.where(low, last, 0)

    def back_term(tile, d):
        pair = jnp.concatenate([cg[d, 2 * tile], cg[d, 2 * tile + 1]], axis=1)
        return jnp.dot(
            wfull[d], pair[:main], preferred_element_type=jnp.float32
        ) + jnp.dot(turned[d], pair[main:], preferred_element_type=jnp.float32)

    def b_copy(mask):
        p = peer(mask)
        return remote(backs.at[p], backr.at[e], b_send.at[mask], b_recv.at[mask], (z, p))

    for i in range(1, parts):
        d = (far + i) % parts
        turned[d] = turn(wtail[d]).astype(jnp.bfloat16)

    @pl.loop(0, 4)
    def _(tile):
        total = back_term(tile, (far + 1) % parts)
        for i in range(2, parts):
            total = total + back_term(tile, (far + i) % parts)
        early[tile] = total

    if last > 1:
        w_step(last, 0)
        w_step(last, 1)
    turned[far] = turn(wtail[far]).astype(jnp.bfloat16)
    for mask in (ALONG_X | ALONG_Y, ALONG_X, ALONG_Y, 0):
        tile = peer(mask) // 2
        total = early[tile] + back_term(tile, far)
        total = total.astype(jnp.bfloat16)
        backs[2 * tile] = total[:, :rows]
        backs[2 * tile + 1] = total[:, rows:]
        if mask:
            b_copy(mask).start()
        b_copy(mask | SIB).start()
    backr[e] = backs[e]

    if last > 2:
        r_farthest(1, False)
        r_rest(1)

    for mask in range(1, 8):
        b_copy(mask).wait_recv()
    for k in range(mine_ref.shape[0]):
        mine = jnp.zeros((tall, rows), jnp.float32)
        for expert in range(8):
            mine = jnp.where(routes[k : k + 1] == expert, backr[expert].astype(jnp.float32), mine)
        mine_ref[k] = mine.astype(jnp.bfloat16)

    def r_end(rightward):
        for q in (0, 1, 2):
            r_wait(z, q, rightward)
            if q == 2:
                came = turn((tail_left if rightward else tail_right)[z])
                part[z, :, main:cols] += came
            else:
                came = (from_left if rightward else from_right)[z, :, lanes[q]]
                part[z, :, lanes[q]] += came.astype(jnp.float32)

    @pl.when(z > 0)
    def _():
        r_end(True)

    @pl.when(z < last)
    def _():
        r_end(False)

    gd_ref[...] = part[z, 0:ffw, :]

    for mask in range(1, 8):
        b_copy(mask).wait_send()
        g_copy(mask).wait_send()
    for unit in range(units):
        for copy in copies[unit]:
            copy.wait_send()
    for q in range(3):
        for hop in range(last):

            @pl.when((z >= hop) & (z < last))
            def _():
                w_copy(hop, q, True).wait_send()

            @pl.when((z + hop <= last) & (z > 0))
            def _():
                w_copy(hop, q, False).wait_send()

        for c in range(parts):

            @pl.when(z < c)
            def _():
                r_copy(c, q, True).wait_send()

            @pl.when(z > c)
            def _():
                r_copy(c, q, False).wait_send()


def fused(grad_out, hidden_act, gate_weights, routing, resp_lengths, advantage, w_down):
    rows, width = grad_out.shape
    ffw = hidden_act.shape[2]
    parts = lax.axis_size("dp")
    cols = width // parts
    tall = round_up(ffw, 16)
    topk = routing.shape[1]
    main = cols // 128 * 128
    tail = cols - main
    responses = resp_lengths.shape
    vmem = pl.BlockSpec(memory_space=pltpu.VMEM)
    hbm = pl.BlockSpec(memory_space=pl.ANY)
    dma = pltpu.SemaphoreType.DMA
    bf16, f32 = jnp.bfloat16, jnp.float32
    total, mine = pl.pallas_call(
        functools.partial(exchange_kernel, parts),
        out_shape=(
            jax.ShapeDtypeStruct((ffw, cols), f32),
            jax.ShapeDtypeStruct((topk, tall, rows), bf16),
        ),
        in_specs=[hbm] * 7,
        out_specs=(vmem, vmem),
        scratch_shapes=[
            pltpu.SMEM(responses, jnp.int32),
            pltpu.SMEM(responses, f32),
            pltpu.VMEM((parts, cols, rows), bf16),
            pltpu.VMEM((topk, ffw, rows), bf16),
            pltpu.VMEM((topk, rows), bf16),
            pltpu.VMEM((topk, rows), jnp.int32),
            pltpu.VMEM((ffw, cols), bf16),
            pltpu.VMEM((parts, 8, cols, rows), bf16),
            pltpu.VMEM((4, tall, 2 * rows), f32),
            pltpu.VMEM((8, tall, rows), bf16),
            pltpu.VMEM((8, tall, rows), bf16),
            pltpu.VMEM((8, tall, rows), bf16),
            pltpu.VMEM((tall, 8 * rows), bf16),
            pltpu.VMEM((parts, tall, main), bf16),
            pltpu.VMEM((parts, tall, cols), f32),
            pltpu.VMEM((parts, tall, main), bf16),
            pltpu.VMEM((parts, tall, main), bf16),
            pltpu.VMEM((parts, tall, main), bf16),
            pltpu.VMEM((8, tall, rows), bf16),
            pltpu.VMEM((parts, tail, tall), bf16),
            pltpu.VMEM((parts, tail, tall), f32),
            pltpu.VMEM((parts, tail, tall), bf16),
            pltpu.VMEM((parts, tail, tall), bf16),
            pltpu.VMEM((parts, tail, tall), bf16),
            pltpu.VMEM((parts, tall, tail), bf16),
            dma((2 * parts, 8)), dma((2 * parts, 8)),
            dma((8,)), dma((8,)),
            dma((2, parts, 3)), dma((2, parts, 3)),
            dma((2, parts, 3)), dma((2, parts, 3)),
            dma((8,)), dma((8,)),
            dma((7,)),
        ],
        compiler_params=pltpu.CompilerParams(
            collective_id=0, has_side_effects=True, vmem_limit_bytes=56 * 1024 * 1024
        ),
        cost_estimate=pl.CostEstimate(
            flops=32 * rows * width * tall, bytes_accessed=8 * rows * width * 2, transcendentals=0
        ),
    )(
        resp_lengths, advantage, grad_out.T.reshape(parts, cols, rows),
        hidden_act.transpose(1, 2, 0), gate_weights.T, routing.T, w_down[0],
    )
    mine = mine[:, :ffw].astype(f32).transpose(2, 0, 1)
    grad_down = total[None]
    grad_gates = jnp.sum(mine * hidden_act.astype(f32), axis=2)
    grad_hidden = gate_weights.astype(f32)[:, :, None] * mine
    return (grad_down, grad_hidden, grad_gates)


def solution(mesh):
    fits = mesh.shape["expert"] == 8 and mesh.shape["dp"] == 4
    body = fused if fits else local

    placed = (
        P(("dp", "expert"), None),
        P(("dp", "expert"), None, None),
        P(("dp", "expert"), None),
        P(("dp", "expert"), None),
        P(("dp", "expert"), None),
        P(("dp", "expert"), None),
        P("expert", None, "dp"),
    )
    return jax.shard_map(
        body,
        mesh=mesh,
        in_specs=placed,
        out_specs=(
            P("expert", None, "dp"),
            P(("dp", "expert"), None, None),
            P(("dp", "expert"), None),
        ),
        check_vma=False,
    )
```
